512 devices in a mesh: lat: 128 (over z, x_lo, y), lon: 4 (over x_hi, core).
Axes of the slice: x: 4 (x_hi: 2, x_lo: 2; x = x_hi * 2 + x_lo), y: 4, z: 16, core: 2. Of those that a mesh axis runs over, the one named last changes fastest.
Arguments:
- tokens: bfloat16 [128, 512, 640], P('lat', 'lon'), may hold values from -6 to 6
- cotangent: bfloat16 [128, 512, 640], P('lat', 'lon'), may hold values from -6 to 6
- raw_obs: bfloat16 [262144, 64], P(('lat', 'lon')), may hold values from -6 to 6
- obs_band: int32 [262144, 1], P(('lat', 'lon')), may hold values from 0 to 127; in each aligned block of 512 rows (0 to 511, 512 to 1023, ...) at most 8 rows name the same one
- obs_slot: int32 [262144], P(('lat', 'lon')), may hold values from 0 to 127
- obs_inst: int32 [262144], P(('lat', 'lon')), may hold values from 0 to 31
- obs_count: int32 [512], P(('lat', 'lon')), may hold values from 256 to 512, as said below
- w_key_obs: bfloat16 [64, 640], replicated, may hold values from -0.75 to 0.75
- w_val_obs: bfloat16 [64, 640], replicated, may hold values from -0.75 to 0.75
- inst_table: bfloat16 [32, 640], replicated, may hold values from -6 to 6
- null_key: bfloat16 [640], replicated, may hold values from -6 to 6
- null_val: bfloat16 [640], replicated, may hold values from -6 to 6
- w_query: bfloat16 [640, 640], replicated, may hold values from -0.25 to 0.25
- norm_gain: float32 [640], replicated, may hold values from 0.1 to 1.9
- zonal_query: bfloat16 [640, 640], replicated, may hold values from -0.25 to 0.25
- zonal_key: bfloat16 [640, 640], replicated, may hold values from -0.25 to 0.25
- zonal_value: bfloat16 [640, 640], replicated, may hold values from -0.25 to 0.25
- zonal_out: bfloat16 [640, 640], replicated, may hold values from -0.25 to 0.25
Outputs:
- d_tokens: bfloat16 [128, 512, 640], P('lat', 'lon')
- key_grad: float32 [64, 640], replicated
- value_grad: float32 [64, 640], replicated
The draws below stay inside these ranges and needn't reach their ends.
Inputs may be any that keep to these rules, and one draw needn't show every extreme that they name: `obs_band`: among the 512 rows of one ingest device, no latitude row is named more than 8 times. The live rows of an ingest device are its first obs_count rows.
All inputs are finite; a program needn't handle non-finite values.
Results may differ from the reference program's by a relative error of at most 0.015.
Values may be sent and summed in bfloat16 or wider, within the bound.
No kernel may reach another device: no remote copies, remote signals or barrier semaphores. Data moves between devices by JAX's collectives and lax.ppermute only.
A program may use at most 128 MiB of HBM per device.

```python
import math
import jax
import jax.numpy as jnp
import numpy as np
from jax import lax

D = 640
HEAD_DIM = 64
FO = 64
NI = 32
LON_DEV = 128
OBS_DEV = 512
LATS = 128
LONS = 512
OBS = 262144
CAP = 8
N_LAT = 128
N_LON = 4
DEVICES = 512


def draw_obs_count(key, part):
    key = jax.random.fold_in(key, 11)
    count_key, pick_key = jax.random.split(key)
    counts = jax.random.randint(count_key, (DEVICES,), OBS_DEV // 2, OBS_DEV + 1)
    chosen = jax.random.randint(pick_key, (), 0, DEVICES)
    return jnp.where(jnp.arange(DEVICES) == chosen, OBS_DEV, counts).astype(jnp.int32)


def touch_ends(drawn, own_key, smallest, high):
    spot = [jax.random.randint(jax.random.fold_in(own_key, axis), (), 0, length) for axis, length in enumerate(drawn.shape)]
    widest = drawn.shape.index(max(drawn.shape))
    next_to = spot[:widest] + [(spot[widest] + 1) % drawn.shape[widest]] + spot[widest + 1:]
    return drawn.at[tuple(spot)].set(smallest).at[tuple(next_to)].set(high)


def steps_of(stream_key, shape, cuts, smallest, top_value):
    loudness, own = 1.0, jax.random.fold_in(stream_key, 6)
    for dim, shards_of in cuts:
        heights = jnp.exp(jax.random.uniform(jax.random.fold_in(own, dim), (shards_of,), jnp.float32, smallest / len(cuts), top_value / len(cuts)))
        loudness = loudness * jnp.repeat(heights, shape[dim] // shards_of).reshape([-1 if axis == dim else 1 for axis in range(len(shape))])
    return loudness


def deal_out(own_key, own, number, rows, number_of, top, bound, slope):
    sequence = jax.random.permutation(own_key, number_of)
    heavy_load, ordinary = portions_of(number_of, rows * top, bound, slope, True), portions_of(number_of, rows * top, bound, slope, False)
    places = jnp.arange(number_of)

    def named(lengths, offset_by):
        used = int((lengths > 0).sum())
        fixed = max(1, used // 4)
        shifted = fixed + (places - fixed + offset_by * (used - fixed)) % max(1, number_of - fixed)
        return jnp.zeros((number_of,), jnp.int32).at[sequence[jnp.where(places < fixed, places, shifted)]].set(jnp.asarray(lengths, jnp.int32))

    lengths = jnp.where(number % 4 == 0, named(heavy_load, number // 4), named(ordinary, number - number // 4 - 1))
    mixed = jax.random.permutation(jax.random.fold_in(own, 3), number_of)
    donor, sink = mixed[0:number_of // 2 * 2:2], mixed[1:number_of // 2 * 2:2]
    slack = jnp.minimum(lengths[donor] - 1, bound - lengths[sink]) // 2
    slack = jnp.where((donor == sequence[0]) | (sink == sequence[0]) | (lengths[sink] == 0), 0, jnp.maximum(slack, 0))
    shifted = jax.random.randint(jax.random.fold_in(own, 4), (number_of // 2,), 0, 1 << 20) % (slack + 1)
    lengths = lengths.at[donor].add(-shifted).at[sink].add(shifted)
    labels = jnp.searchsorted(jnp.cumsum(lengths), jnp.arange(rows * top), side="right").astype(jnp.int32)
    table = labels.reshape(top, rows).T
    table = table[jax.random.permutation(jax.random.fold_in(own, 1), rows)]
    offset_by = jax.random.randint(jax.random.fold_in(own, 2), (rows, 1), 0, top)
    return jnp.take_along_axis(table, (jnp.arange(top)[None, :] + offset_by) % top, axis=1)


def portions_of(count, total, most, skew, full):
    loads = [(1 << 20) // math.isqrt(grade ** skew) + 1 for grade in range(1, count + 1)]
    largest = most if full else min(most, max(-(-total // count), total * loads[0] // sum(loads)))
    least = 1 if total - largest >= count - 1 else 0
    given, surplus = [largest] + [least] * (count - 1), total - largest - least * (count - 1)
    while surplus > 0:
        candidates = [i for i in range(1, count) if given[i] < largest] or [i for i in range(1, count) if given[i] < most]
        whole, budget = sum([loads[i] for i in candidates]), surplus
        for i in candidates:
            addition = min(most - given[i], max(1, budget * loads[i] // whole), surplus)
            given[i] = given[i] + addition
            surplus = surplus - addition
    return np.array(given)


def noise(stream_key, extent, scale, bound, cuts=(), kind=jnp.bfloat16):
    gain = steps_of(stream_key, extent, cuts, -0.22, 0.18) if cuts else 1.0
    entries = jax.random.normal(stream_key, extent, jnp.float32) * scale * gain
    return jnp.minimum(jnp.maximum(entries, -bound), bound).astype(kind)


def setup_inputs(seed: int = 0) -> dict:
    streams_of = jax.random.split(jax.random.key(seed), 19)
    tokens = noise(streams_of[0], (LATS, LONS, D), 1.0, 6.0, ((0, 128), (1, 4)))
    cotangent = noise(streams_of[1], (LATS, LONS, D), 1.0, 6.0, ((0, 128), (1, 4)))
    raw_obs = noise(streams_of[2], (OBS, FO), 1.0, 6.0, ((0, 512),))
    obs_band_keys = jax.random.split(jax.random.fold_in(streams_of[3], 1), OBS // OBS_DEV)
    obs_band_turns = jax.random.permutation(jax.random.fold_in(streams_of[3], 3), OBS // OBS_DEV)
    obs_band = jax.vmap(lambda own, number: deal_out(jax.random.fold_in(streams_of[3], 2), own, number, OBS_DEV, N_LAT, 1, CAP, 2))(obs_band_keys, obs_band_turns).reshape((OBS, 1))
    obs_slot = touch_ends(jax.random.randint(streams_of[4], (OBS,), 0, LON_DEV), jax.random.fold_in(streams_of[4], 1), 0, LON_DEV - 1).astype(jnp.int32)
    obs_inst = touch_ends(jax.random.randint(streams_of[5], (OBS,), 0, NI), jax.random.fold_in(streams_of[5], 1), 0, NI - 1).astype(jnp.int32)
    obs_count = draw_obs_count(jax.random.fold_in(streams_of[18], 71), 0)
    w_key_obs = noise(streams_of[7], (FO, D), FO ** -0.5, 0.75)
    w_val_obs = noise(streams_of[8], (FO, D), FO ** -0.5, 0.75)
    inst_table = noise(streams_of[9], (NI, D), 1.0, 6.0)
    null_key = noise(streams_of[10], (D,), 1.0, 6.0)
    null_val = noise(streams_of[11], (D,), 1.0, 6.0)
    w_query = noise(streams_of[12], (D, D), D ** -0.5, 0.25)
    norm_gain = jnp.clip(1.0 + 0.18 * jax.random.normal(streams_of[13], (D,), jnp.float32), 0.1, 1.9)
    zonal_query = noise(streams_of[14], (D, D), D ** -0.5, 0.25)
    zonal_key = noise(streams_of[15], (D, D), D ** -0.5, 0.25)
    zonal_value = noise(streams_of[16], (D, D), D ** -0.5, 0.25)
    zonal_out = noise(streams_of[17], (D, D), D ** -0.5, 0.25)
    return dict(tokens=tokens, cotangent=cotangent, raw_obs=raw_obs, obs_band=obs_band, obs_slot=obs_slot, obs_inst=obs_inst, obs_count=obs_count, w_key_obs=w_key_obs, w_val_obs=w_val_obs, inst_table=inst_table, null_key=null_key, null_val=null_val, w_query=w_query, norm_gain=norm_gain, zonal_query=zonal_query, zonal_key=zonal_key, zonal_value=zonal_value, zonal_out=zonal_out)


logit_cap = 6.0
norm_eps = 1e-06

def capped(raw_score):
    return logit_cap * jnp.tanh(raw_score / logit_cap)

def cap_slope(raw_score):
    inner_tanh = jnp.tanh(raw_score / logit_cap)
    return 1.0 - inner_tanh * inner_tanh

def silu_slope(value):
    sigma = jax.nn.sigmoid(value)
    return sigma * (1.0 + value * (1.0 - sigma))

def encode(raw_rows, inst_rows, w_key_obs, w_val_obs, inst_table):
    obs_keys = jnp.dot(raw_rows, w_key_obs, preferred_element_type=jnp.float32).astype(jnp.bfloat16)
    inst_hot = (inst_rows[:, None] == jnp.arange(inst_table.shape[0], dtype=jnp.int32)[None, :]).astype(jnp.bfloat16)
    pre_values = jnp.dot(raw_rows, w_val_obs, preferred_element_type=jnp.float32) + jnp.dot(inst_hot, inst_table, preferred_element_type=jnp.float32)
    obs_values = jax.nn.silu(pre_values).astype(jnp.bfloat16)
    return (obs_keys, obs_values, pre_values)

def times_transposed(left, weight):
    return lax.dot_general(left, weight, (((1,), (1,)), ((), ())), preferred_element_type=jnp.float32)

def rms_backward(resid_f, inverse, norm_gain, d_normed, cotangent_f):
    gained = norm_gain.astype(jnp.float32) * d_normed
    return cotangent_f + inverse * gained - resid_f * inverse ** 3 * lax.optimization_barrier(jnp.mean(resid_f * gained, axis=-1, keepdims=True))

def zonal_backward(zq_rows, zk_all, zv_all, d_att, head_dim):
    count_q = zq_rows.shape[0]
    count_k = zk_all.shape[0]
    head_count = zq_rows.shape[1] // head_dim
    score_scale = 1.0 / math.sqrt(head_dim)
    q_heads = zq_rows.astype(jnp.float32).reshape(count_q, head_count, head_dim)
    k_heads = zk_all.astype(jnp.float32).reshape(count_k, head_count, head_dim)
    v_heads = zv_all.astype(jnp.float32).reshape(count_k, head_count, head_dim)
    a_heads = d_att.astype(jnp.float32).reshape(count_q, head_count, head_dim)
    raw_score = jnp.einsum('phd,lhd->hpl', q_heads, k_heads) * score_scale
    weight_z = jnp.exp(capped(raw_score))
    prob_f = weight_z / lax.optimization_barrier(jnp.sum(weight_z, axis=2, keepdims=True))
    prob_b = prob_f.astype(jnp.bfloat16)
    d_prob = jnp.einsum('phd,lhd->hpl', a_heads, v_heads)
    inner_sum = lax.optimization_barrier(jnp.sum(prob_f * d_prob, axis=2, keepdims=True))
    d_raw = (prob_f * (d_prob - inner_sum) * cap_slope(raw_score) * score_scale).astype(jnp.bfloat16)
    d_query = jnp.einsum('hpl,lhd->phd', d_raw.astype(jnp.float32), k_heads).astype(jnp.bfloat16).reshape(count_q, -1)
    key_term = jnp.einsum('hpl,phd->lhd', d_raw.astype(jnp.float32), q_heads).reshape(count_k, -1)
    value_term = jnp.einsum('hpl,phd->lhd', prob_b.astype(jnp.float32), a_heads).reshape(count_k, -1)
    return (d_query, key_term, value_term)

def reference(tokens, cotangent, raw_obs, obs_band, obs_slot, obs_inst, obs_count, w_key_obs, w_val_obs, inst_table, null_key, null_val, w_query, norm_gain, zonal_query, zonal_key, zonal_value, zonal_out):
    head_count = D // HEAD_DIM
    score_scale = 1.0 / math.sqrt(HEAD_DIM)
    resid_in = tokens.reshape(-1, D)
    cotangent_rows = cotangent.reshape(-1, D)
    token_total = resid_in.shape[0]
    obs_total = raw_obs.shape[0]
    row_order = jnp.arange(obs_total, dtype=jnp.int32)
    device_of = row_order // OBS_DEV
    live_rows = row_order % OBS_DEV < obs_count[device_of]
    token_of = (obs_band[:, 0] * LONS + device_of % N_LON * LON_DEV + obs_slot).astype(jnp.int32)
    obs_keys, obs_values, pre_values = encode(raw_obs, obs_inst, w_key_obs, w_val_obs, inst_table)
    query_rows = jnp.dot(resid_in, w_query, preferred_element_type=jnp.float32).astype(jnp.bfloat16)
    q_heads = query_rows.astype(jnp.float32).reshape(token_total, head_count, HEAD_DIM)
    q_obs = q_heads[token_of]
    k_obs = obs_keys.astype(jnp.float32).reshape(obs_total, head_count, HEAD_DIM)
    v_obs = obs_values.astype(jnp.float32).reshape(obs_total, head_count, HEAD_DIM)
    null_k = null_key.astype(jnp.float32).reshape(head_count, HEAD_DIM)
    null_v = null_val.astype(jnp.float32).reshape(head_count, HEAD_DIM)
    raw_cross = lax.optimization_barrier(jnp.sum(q_obs * k_obs, axis=2)) * score_scale
    weight_cross = jnp.where(live_rows[:, None], jnp.exp(capped(raw_cross)), 0.0)
    raw_null = lax.optimization_barrier(jnp.sum(q_heads * null_k, axis=2)) * score_scale
    weight_null = jnp.exp(capped(raw_null))
    total_cross = weight_null + jax.ops.segment_sum(weight_cross, token_of, num_segments=token_total)
    prob_cross = weight_cross / total_cross[token_of]
    prob_null = weight_null / total_cross
    prob_cross_b = prob_cross.astype(jnp.bfloat16).astype(jnp.float32)
    prob_null_b = prob_null.astype(jnp.bfloat16).astype(jnp.float32)
    gathered = jax.ops.segment_sum((prob_cross_b[:, :, None] * v_obs).reshape(obs_total, D), token_of, num_segments=token_total)
    gathered = gathered + (prob_null_b[:, :, None] * null_v).reshape(token_total, D)
    resid_mid = (resid_in.astype(jnp.float32) + gathered).astype(jnp.bfloat16)
    resid_f = resid_mid.astype(jnp.float32)
    inverse = lax.rsqrt(lax.optimization_barrier(jnp.mean(resid_f * resid_f, axis=1, keepdims=True)) + norm_eps)
    normed = (resid_f * inverse * norm_gain.astype(jnp.float32)).astype(jnp.bfloat16)
    zonal_q = jnp.dot(normed, zonal_query, preferred_element_type=jnp.float32).astype(jnp.bfloat16)
    zonal_k = jnp.dot(normed, zonal_key, preferred_element_type=jnp.float32).astype(jnp.bfloat16)
    zonal_v = jnp.dot(normed, zonal_value, preferred_element_type=jnp.float32).astype(jnp.bfloat16)
    d_att = times_transposed(cotangent_rows, zonal_out).astype(jnp.bfloat16)

    def one_row(pieces):
        q_row, k_row, v_row, a_row = pieces
        d_q, key_term, value_term = zonal_backward(q_row, k_row, v_row, a_row, HEAD_DIM)
        return (d_q, key_term.astype(jnp.bfloat16), value_term.astype(jnp.bfloat16))
    shaped = (zonal_q.reshape(LATS, LONS, D), zonal_k.reshape(LATS, LONS, D), zonal_v.reshape(LATS, LONS, D), d_att.reshape(LATS, LONS, D))
    d_zq, d_zk, d_zv = lax.map(one_row, shaped)
    d_normed = times_transposed(d_zq.reshape(-1, D), zonal_query) + times_transposed(d_zk.reshape(-1, D), zonal_key) + times_transposed(d_zv.reshape(-1, D), zonal_value)
    d_resid = rms_backward(resid_f, inverse, norm_gain, d_normed, cotangent_rows.astype(jnp.float32)).astype(jnp.bfloat16)
    d_heads = d_resid.astype(jnp.float32).reshape(token_total, head_count, HEAD_DIM)
    d_obs = d_heads[token_of]
    d_prob = lax.optimization_barrier(jnp.sum(d_obs * v_obs, axis=2))
    d_prob_null = lax.optimization_barrier(jnp.sum(d_heads * null_v, axis=2))
    inner_cross = prob_null * d_prob_null + jax.ops.segment_sum(prob_cross * d_prob, token_of, num_segments=token_total)
    d_raw = (prob_cross * (d_prob - inner_cross[token_of]) * cap_slope(raw_cross) * score_scale).astype(jnp.bfloat16)
    d_raw_null = prob_null * (d_prob_null - inner_cross) * cap_slope(raw_null) * score_scale
    d_raw_f = d_raw.astype(jnp.float32)
    d_query = jax.ops.segment_sum((d_raw_f[:, :, None] * k_obs).reshape(obs_total, D), token_of, num_segments=token_total)
    d_query = (d_query + (d_raw_null[:, :, None] * null_k).reshape(token_total, D)).astype(jnp.bfloat16)
    d_tokens = (d_resid.astype(jnp.float32) + times_transposed(d_query, w_query)).astype(jnp.bfloat16)
    d_keys = (d_raw_f[:, :, None] * q_obs).reshape(obs_total, D).astype(jnp.bfloat16)
    d_values = (prob_cross_b[:, :, None] * d_obs).reshape(obs_total, D).astype(jnp.bfloat16)
    d_pre = (d_values.astype(jnp.float32) * silu_slope(pre_values)).astype(jnp.bfloat16)
    obs_norm = 1.0 / math.sqrt(obs_total)
    key_grad = lax.dot_general(raw_obs, d_keys, (((0,), (0,)), ((), ())), preferred_element_type=jnp.float32) * obs_norm
    value_grad = lax.dot_general(raw_obs, d_pre, (((0,), (0,)), ((), ())), preferred_element_type=jnp.float32) * obs_norm
    return (d_tokens.reshape(tokens.shape), key_grad, value_grad)
```

```python
import math

import jax
import jax.numpy as jnp
from jax import lax
from jax.experimental import pallas as pl
from jax.experimental.pallas import tpu as pltpu
from jax.sharding import PartitionSpec as P

HEAD_DIM = 64
CAP_ROWS = 8
LANES = 128
FEATS = 64

logit_cap = 6.0
norm_eps = 1e-06
score_scale = 1.0 / math.sqrt(HEAD_DIM)

bf16 = jnp.bfloat16
f32 = jnp.float32
i32 = jnp.int32

PLANE = 32
DEPTH = 16
CHUNK = 24
ROW_BLOCK = 256


def iota(shape, dim):
    return lax.broadcasted_iota(i32, shape, dim)


def dot_nn(a, b):
    return lax.dot_general(a, b, (((1,), (0,)), ((), ())), preferred_element_type=f32)


def dot_nt(a, b):
    return lax.dot_general(a, b, (((1,), (1,)), ((), ())), preferred_element_type=f32)


def dot_tn(a, b):
    return lax.dot_general(a, b, (((0,), (0,)), ((), ())), preferred_element_type=f32)


def halves(value):
    high = value.astype(bf16)
    return high, (value - high.astype(f32)).astype(bf16)


def fine_nn(a, value):
    high, low = halves(value)
    return dot_nn(a, high) + dot_nn(a, low)


def fine_tn(a, value):
    high, low = halves(value)
    return dot_tn(a, high) + dot_tn(a, low)


def head_sum_matrix(width):
    return jnp.where(
        iota((width, LANES), 0) // HEAD_DIM == iota((width, LANES), 1), 1.0, 0.0
    ).astype(bf16)


def head_spread_matrix(width):
    return jnp.where(
        iota((LANES, width), 1) // HEAD_DIM == iota((LANES, width), 0), 1.0, 0.0
    ).astype(bf16)


def token_hot(x_rows):
    slot = x_rows[:, FEATS : FEATS + 1].astype(f32).astype(i32)
    return jnp.where(iota((x_rows.shape[0], LANES), 1) == slot - 1, 1.0, 0.0).astype(bf16)


def pack_kernel(count_ref, band_ref, slot_ref, inst_ref, raw_ref, out_ref):
    rows = band_ref.shape[1]
    slots = out_ref.shape[0]
    bands = slots // CAP_ROWS
    band = band_ref[...]
    live = iota((1, rows), 1) < count_ref[0]
    dest = jnp.where(live, band, -1)
    named = iota((bands, rows), 0) == dest
    hot = jnp.where(named, 1.0, 0.0).astype(bf16)
    earlier = jnp.where(iota((rows, rows), 0) < iota((rows, rows), 1), 1.0, 0.0).astype(bf16)
    before = dot_nn(hot, earlier)
    rank = jnp.sum(jnp.where(named, before, 0.0), axis=0, keepdims=True).astype(i32)
    position = jnp.where(live, band * CAP_ROWS + rank, -1)
    pick = jnp.where(iota((slots, rows), 0) == position, 1.0, 0.0).astype(bf16)
    part = iota((LANES - FEATS, rows), 0)
    meta = jnp.where(
        part == 0,
        (slot_ref[...] + 1).astype(f32),
        jnp.where(part == 1, inst_ref[...].astype(f32), 0.0),
    ).astype(bf16)
    payload = jnp.concatenate([raw_ref[...], meta], axis=0)
    out_ref[...] = dot_nt(pick, payload).astype(bf16)


def cross_kernel(
    x_ref,
    query_ref,
    tok_ref,
    wk_ref,
    wv_ref,
    table_ref,
    nk_ref,
    nv_ref,
    gain_ref,
    resid_ref,
    normed_ref,
    key_ref,
    val_ref,
    slope_ref,
    qs_ref,
    tanh_ref,
    prob_ref,
    ntanh_ref,
    nprob_ref,
    hot_s,
    weight_s,
):
    slots = x_ref.shape[0]
    toks, width = tok_ref.shape
    pad = jnp.zeros((LANES - FEATS, width), bf16)
    w_key = jnp.concatenate([wk_ref[...], pad], axis=0)
    w_val = jnp.concatenate(
        [wv_ref[...], pad, table_ref[...], jnp.zeros((LANES - table_ref.shape[0], width), bf16)],
        axis=0,
    )
    head_sum = head_sum_matrix(width)
    head_spread = head_spread_matrix(width)
    query = query_ref[...]
    total = jnp.zeros((toks, LANES), f32)
    for start in range(0, slots, ROW_BLOCK):
        span = pl.ds(start, ROW_BLOCK)
        x = x_ref[span, :]
        hot = token_hot(x)
        hot_s[span, :] = hot
        inst = x[:, FEATS + 1 : FEATS + 2].astype(f32).astype(i32)
        inst_hot = jnp.where(iota((ROW_BLOCK, LANES), 1) == inst, 1.0, 0.0).astype(bf16)
        keys = dot_nn(x, w_key).astype(bf16)
        key_ref[span, :] = keys
        pre = dot_nn(jnp.concatenate([x, inst_hot], axis=1), w_val)
        sigma = 1.0 / (1.0 + jnp.exp(-pre))
        val_ref[span, :] = (pre * sigma).astype(bf16)
        slope_ref[span, :] = (sigma * (1.0 + pre * (1.0 - sigma))).astype(bf16)
        q_slot = dot_nn(hot, query).astype(bf16)
        qs_ref[span, :] = q_slot
        t = jnp.tanh(dot_nn(q_slot * keys, head_sum) * (score_scale / logit_cap))
        tanh_ref[span, :] = t
        weight = jnp.exp(logit_cap * t)
        weight_s[span, :] = weight
        total = total + fine_tn(hot, weight)
    null_t = jnp.tanh(
        fine_nn_left(query.astype(f32) * nk_ref[...].astype(f32), head_sum)
        * (score_scale / logit_cap)
    )
    null_weight = jnp.exp(logit_cap * null_t)
    share = 1.0 / (total + null_weight)
    null_prob = null_weight * share
    ntanh_ref[...] = null_t
    nprob_ref[...] = null_prob
    gathered = dot_nn(null_prob.astype(bf16), head_spread) * nv_ref[...].astype(f32)
    for start in range(0, slots, ROW_BLOCK):
        span = pl.ds(start, ROW_BLOCK)
        hot = hot_s[span, :]
        prob = weight_s[span, :] * fine_nn(hot, share)
        prob_ref[span, :] = prob
        spread = dot_nn(prob.astype(bf16), head_spread).astype(bf16)
        gathered = gathered + dot_tn(hot, spread * val_ref[span, :])
    resid = (tok_ref[...].astype(f32) + gathered).astype(bf16)
    resid_ref[...] = resid
    resid_f = resid.astype(f32)
    inverse = lax.rsqrt(jnp.mean(resid_f * resid_f, axis=1, keepdims=True) + norm_eps)
    normed_ref[...] = (resid_f * inverse * gain_ref[...]).astype(bf16)


def fine_nn_left(value, b):
    high, low = halves(value)
    return dot_nn(high, b) + dot_nn(low, b)


def zonal_kernel(
    me_ref,
    normed_ref,
    att_ref,
    zq_ref,
    zk_ref,
    zv_ref,
    resid_ref,
    cot_ref,
    gain_ref,
    dres_ref,
    zq_s,
    zk_s,
    zkt_s,
    zv_s,
    att_s,
    norm_s,
    dq_s,
    dk_s,
    dv_s,
):
    whole, width = normed_ref.shape
    own = resid_ref.shape[0]
    sectors = whole // own
    pairs = width // LANES
    me = me_ref[0]
    for k in range(sectors):
        src = pl.multiple_of(lax.rem(me + k, sectors) * own, own)
        norm_s[k * own : (k + 1) * own, :] = normed_ref[pl.ds(src, own), :]
        part = att_ref[pl.ds(src, own), :]
        for p in range(pairs):
            att_s[p, k * own : (k + 1) * own, :] = part[:, p * LANES : (p + 1) * LANES]
    normed = norm_s[...]
    for ref, out in ((zq_ref, zq_s), (zk_ref, zk_s), (zv_ref, zv_s)):
        proj = dot_nn(normed, ref[...])
        for p in range(pairs):
            piece = proj[:, p * LANES : (p + 1) * LANES]
            out[p] = piece.astype(bf16)
            if out is zk_s:
                zkt_s[p] = piece.T.astype(bf16)
    lane_head = iota((whole, LANES), 1) // HEAD_DIM
    step = 2 * own

    def one_pair(p, carry):
        keys = zk_s[p]
        vals = zv_s[p]
        dk = jnp.zeros((own, LANES), f32)
        dv = jnp.zeros((own, LANES), f32)
        for head in range(2):
            qm = jnp.where(lane_head == head, zq_s[p], jnp.zeros((), bf16))
            am = jnp.where(lane_head == head, att_s[p], jnp.zeros((), bf16))
            for start in range(0, whole, step):
                q_part = qm[start : start + step]
                a_part = am[start : start + step]
                t = jnp.tanh(dot_nt(keys, q_part) * (score_scale / logit_cap))
                zdp = dot_nt(vals, a_part)
                weight = jnp.exp(logit_cap * t)
                share = 1.0 / jnp.sum(weight, axis=0, keepdims=True)
                inner = jnp.sum(weight * zdp, axis=0, keepdims=True) * share
                scaled = share * score_scale

                def d_raw_of(rows, cols):
                    tt = t[rows, cols]
                    return (
                        weight[rows, cols]
                        * scaled[:, cols]
                        * (zdp[rows, cols] - inner[:, cols])
                        * (1.0 - tt * tt)
                    ).astype(bf16)

                top = d_raw_of(slice(0, own), slice(None))
                prob = (weight[:own] * share).astype(bf16)
                dk = dk + dot_nn(top, q_part)
                dv = dv + dot_nn(prob, a_part)
                if start == 0:
                    rest = d_raw_of(slice(own, None), slice(0, own))
                    column = jnp.concatenate([top[:, :own], rest], axis=0)
                    keys_t = zkt_s[p, head * HEAD_DIM : (head + 1) * HEAD_DIM, :]
                    dq_s[p, head * HEAD_DIM : (head + 1) * HEAD_DIM, :] = dot_nn(keys_t, column)
        dk_s[p] = dk.astype(bf16)
        dv_s[p] = dv.astype(bf16)
        return carry

    lax.fori_loop(0, pairs, one_pair, 0)
    d_normed = jnp.zeros((own, width), f32)
    for p in range(pairs):
        cols = slice(p * LANES, (p + 1) * LANES)
        d_normed = d_normed + dot_nt(dq_s[p].T.astype(bf16), zq_ref[:, cols])
        d_normed = d_normed + dot_nt(dk_s[p], zk_ref[:, cols])
        d_normed = d_normed + dot_nt(dv_s[p], zv_ref[:, cols])
    resid_f = resid_ref[...].astype(f32)
    inverse = lax.rsqrt(jnp.mean(resid_f * resid_f, axis=1, keepdims=True) + norm_eps)
    gained = gain_ref[...] * d_normed
    dres_ref[...] = (
        cot_ref[...].astype(f32)
        + inverse * gained
        - resid_f * (inverse * inverse * inverse) * jnp.mean(resid_f * gained, axis=1, keepdims=True)
    ).astype(bf16)


def back_kernel(
    x_ref,
    dres_ref,
    wq_ref,
    nk_ref,
    nv_ref,
    key_ref,
    val_ref,
    slope_ref,
    qs_ref,
    tanh_ref,
    prob_ref,
    ntanh_ref,
    nprob_ref,
    dtok_ref,
    grad_ref,
    ds_s,
    dp_s,
):
    slots = x_ref.shape[0]
    toks, width = dres_ref.shape
    head_sum = head_sum_matrix(width)
    head_spread = head_spread_matrix(width)
    d_resid = dres_ref[...]
    null_prob = nprob_ref[...]
    null_t = ntanh_ref[...]
    null_dp = fine_nn_left(d_resid.astype(f32) * nv_ref[...].astype(f32), head_sum)
    inner = null_prob * null_dp
    for start in range(0, slots, ROW_BLOCK):
        span = pl.ds(start, ROW_BLOCK)
        hot = token_hot(x_ref[span, :])
        d_slot = dot_nn(hot, d_resid).astype(bf16)
        ds_s[span, :] = d_slot
        dp = dot_nn(d_slot * val_ref[span, :], head_sum)
        dp_s[span, :] = dp
        inner = inner + fine_tn(hot, prob_ref[span, :] * dp)
    null_raw = null_prob * (null_dp - inner) * (1.0 - null_t * null_t) * score_scale
    d_query = fine_nn_left(null_raw, head_spread) * nk_ref[...].astype(f32)
    grads = jnp.zeros((LANES, 2 * width), f32)
    for start in range(0, slots, ROW_BLOCK):
        span = pl.ds(start, ROW_BLOCK)
        x = x_ref[span, :]
        hot = token_hot(x)
        prob = prob_ref[span, :]
        t = tanh_ref[span, :]
        d_raw = (
            prob * (dp_s[span, :] - fine_nn(hot, inner)) * (1.0 - t * t) * score_scale
        ).astype(bf16)
        d_raw_wide = dot_nn(d_raw, head_spread).astype(bf16)
        prob_wide = dot_nn(prob.astype(bf16), head_spread).astype(bf16)
        d_query = d_query + dot_tn(hot, d_raw_wide * key_ref[span, :])
        d_keys = d_raw_wide * qs_ref[span, :]
        d_pre = (prob_wide * ds_s[span, :]) * slope_ref[span, :]
        grads = grads + dot_tn(x, jnp.concatenate([d_keys, d_pre], axis=1))
    d_tok = d_resid.astype(f32) + dot_nt(d_query.astype(bf16), wq_ref[...])
    dtok_ref[...] = d_tok.astype(bf16)
    blocks = 2 * width // LANES
    for b in range(blocks):
        grad_ref[b * FEATS : (b + 1) * FEATS, :] = grads[
            :FEATS, b * LANES : (b + 1) * LANES
        ].astype(bf16)
    spare = grad_ref.shape[0] - blocks * FEATS
    grad_ref[blocks * FEATS :, :] = jnp.zeros((spare, LANES), bf16)


def whole_call(kernel, name, out_shape, args, scalars=0, scratch=()):
    vmem = pl.BlockSpec(memory_space=pltpu.VMEM)
    smem = pl.BlockSpec(memory_space=pltpu.SMEM)
    return pl.pallas_call(
        kernel,
        name=name,
        out_shape=out_shape,
        in_specs=[smem] * scalars + [vmem] * (len(args) - scalars),
        out_specs=[vmem] * len(out_shape) if isinstance(out_shape, (list, tuple)) else vmem,
        scratch_shapes=list(scratch),
        compiler_params=pltpu.CompilerParams(vmem_limit_bytes=56 * 1024 * 1024),
    )(*args)


def shaped(rows, cols, dtype):
    return jax.ShapeDtypeStruct((rows, cols), dtype)


def pack(obs_count, obs_band, obs_slot, obs_inst, raw_obs, bands):
    rows = raw_obs.shape[0]
    return whole_call(
        pack_kernel,
        "pack",
        shaped(bands * CAP_ROWS, LANES, bf16),
        (
            obs_count,
            obs_band.reshape(1, rows),
            obs_slot.reshape(1, rows),
            obs_inst.reshape(1, rows),
            raw_obs.T,
        ),
        scalars=1,
    )


def cross_forward(x, query, tok, w_key, w_val, table, null_key, null_val, gain):
    slots = x.shape[0]
    toks, width = tok.shape
    big = shaped(slots, width, bf16)
    small = shaped(slots, LANES, f32)
    null = shaped(toks, LANES, f32)
    row = shaped(toks, width, bf16)
    return whole_call(
        cross_kernel,
        "cross_forward",
        [row, row, big, big, big, big, small, small, null, null],
        (x, query, tok, w_key, w_val, table, null_key, null_val, gain),
        scratch=(pltpu.VMEM((slots, LANES), bf16), pltpu.VMEM((slots, LANES), f32)),
    )


def zonal(me, normed_all, att_all, zq, zk, zv, resid, cot, gain):
    own, width = resid.shape
    whole = normed_all.shape[0]
    pairs = width // LANES
    rows = pltpu.VMEM((pairs, whole, LANES), bf16)
    return whole_call(
        zonal_kernel,
        "zonal",
        shaped(own, width, bf16),
        (me, normed_all, att_all, zq, zk, zv, resid, cot, gain),
        scalars=1,
        scratch=(
            rows,
            rows,
            pltpu.VMEM((pairs, LANES, whole), bf16),
            rows,
            rows,
            pltpu.VMEM((whole, width), bf16),
            pltpu.VMEM((pairs, LANES, own), f32),
            pltpu.VMEM((pairs, own, LANES), bf16),
            pltpu.VMEM((pairs, own, LANES), bf16),
        ),
    )


def cross_backward(x, d_resid, w_query, null_key, null_val, saved):
    slots = x.shape[0]
    toks, width = d_resid.shape
    return whole_call(
        back_kernel,
        "cross_backward",
        [shaped(toks, width, bf16), shaped(PLANE * CHUNK, LANES, bf16)],
        (x, d_resid, w_query, null_key, null_val) + tuple(saved),
        scratch=(pltpu.VMEM((slots, width), bf16), pltpu.VMEM((slots, LANES), f32)),
    )


def sum_everywhere(rows):
    plane = [list(range(z * PLANE, (z + 1) * PLANE)) for z in range(DEPTH)]
    lats = PLANE // 4
    column = [[z * lats + k for z in range(DEPTH)] for k in range(lats)]

    def swap(parts, axes, groups):
        return lax.all_to_all(
            parts, axes, split_axis=0, concat_axis=0, tiled=True, axis_index_groups=groups
        )

    def total(parts):
        return jnp.sum(parts.astype(f32), axis=0)

    parts = swap(rows.reshape(PLANE, CHUNK, LANES), ("lat", "lon"), plane)
    mine = total(parts).astype(bf16)
    parts = swap(jnp.broadcast_to(mine, (DEPTH, CHUNK, LANES)), "lat", column)
    mine = total(parts).astype(bf16)
    parts = swap(jnp.broadcast_to(mine, (PLANE, CHUNK, LANES)), ("lat", "lon"), plane)
    return parts.reshape(PLANE * CHUNK, LANES)


def on_device(
    tokens,
    cotangent,
    raw_obs,
    obs_band,
    obs_slot,
    obs_inst,
    obs_count,
    w_key_obs,
    w_val_obs,
    inst_table,
    null_key,
    null_val,
    w_query,
    norm_gain,
    zonal_query,
    zonal_key,
    zonal_value,
    zonal_out,
):
    tok_rows, width = tokens.shape[1:]
    bands = lax.axis_size("lat")
    devices = bands * lax.axis_size("lon")
    obs_total = raw_obs.shape[0] * devices
    tok = tokens.reshape(tok_rows, width)
    cot = cotangent.reshape(tok_rows, width)
    null_key = null_key.reshape(1, width)
    null_val = null_val.reshape(1, width)
    gain = norm_gain.reshape(1, width)
    packed = pack(obs_count, obs_band, obs_slot, obs_inst, raw_obs, bands)
    received = lax.all_to_all(
        packed.reshape(bands, CAP_ROWS, LANES), "lat", split_axis=0, concat_axis=0, tiled=True
    ).reshape(bands * CAP_ROWS, LANES)
    query = jnp.dot(tok, w_query, preferred_element_type=f32).astype(bf16)
    d_att = dot_nt(cot, zonal_out).astype(bf16)
    att_all = lax.all_gather(d_att, "lon", axis=0, tiled=True)
    resid, normed, *saved = cross_forward(
        received, query, tok, w_key_obs, w_val_obs, inst_table, null_key, null_val, gain
    )
    normed_all = lax.all_gather(normed, "lon", axis=0, tiled=True)
    me = lax.axis_index("lon").astype(i32).reshape(1)
    d_resid = zonal(
        me, normed_all, att_all, zonal_query, zonal_key, zonal_value, resid, cot, gain
    )
    d_tok, grads = cross_backward(received, d_resid, w_query, null_key, null_val, saved)
    summed = sum_everywhere(grads)[: 2 * FEATS * width // LANES]
    summed = summed.astype(f32) * (1.0 / math.sqrt(obs_total))
    summed = summed.reshape(2, width // LANES, FEATS, LANES).transpose(0, 2, 1, 3)
    summed = summed.reshape(2, FEATS, width)
    return d_tok.reshape(1, tok_rows, width), summed[0], summed[1]


def solution(mesh):
    return jax.shard_map(
        on_device,
        mesh=mesh,
        in_specs=(
            P("lat", "lon", None),
            P("lat", "lon", None),
            P(("lat", "lon"), None),
            P(("lat", "lon"), None),
            P(("lat", "lon")),
            P(("lat", "lon")),
            P(("lat", "lon")),
            P(),
            P(),
            P(),
            P(),
            P(),
            P(),
            P(),
            P(),
            P(),
            P(),
            P(),
        ),
        out_specs=(P("lat", "lon", None), P(), P()),
        check_vma=False,
    )
```

```python
import functools
import math

import jax
import jax.numpy as jnp
from jax import lax
from jax.experimental import pallas as pl
from jax.experimental.pallas import tpu as pltpu
from jax.sharding import PartitionSpec as P

HEAD_DIM = 64
CAP_ROWS = 8
LANES = 128
FEATS = 64

logit_cap = 6.0
norm_eps = 1e-06
score_scale = 1.0 / math.sqrt(HEAD_DIM)

bf16 = jnp.bfloat16
f32 = jnp.float32
i32 = jnp.int32

PLANE = 32
DEPTH = 16
CHUNK = 24
ROW_BLOCK = 256


def iota(shape, dim):
    return lax.broadcasted_iota(i32, shape, dim)


def dot_nn(a, b):
    return lax.dot_general(a, b, (((1,), (0,)), ((), ())), preferred_element_type=f32)


def dot_nt(a, b):
    return lax.dot_general(a, b, (((1,), (1,)), ((), ())), preferred_element_type=f32)


def dot_tn(a, b):
    return lax.dot_general(a, b, (((0,), (0,)), ((), ())), preferred_element_type=f32)


def halves(value):
    high = value.astype(bf16)
    return high, (value - high.astype(f32)).astype(bf16)


def fine_nn(twice, value):
    return dot_nn(twice, jnp.concatenate(halves(value), axis=0))


def fine_tn(a, value):
    both = dot_tn(a, jnp.concatenate(halves(value), axis=1))
    return both[:, : value.shape[1]] + both[:, value.shape[1] :]


def fine_nn_left(value, b):
    high, low = halves(value)
    return dot_nn(high, b) + dot_nn(low, b)


def doubled(hot):
    return jnp.concatenate([hot, hot], axis=1)


def head_sum_matrix(width):
    return jnp.where(
        iota((width, LANES), 0) // HEAD_DIM == iota((width, LANES), 1), 1.0, 0.0
    ).astype(bf16)


def head_spread_matrix(width):
    return jnp.where(
        iota((LANES, width), 1) // HEAD_DIM == iota((LANES, width), 0), 1.0, 0.0
    ).astype(bf16)


def token_hot(x_rows):
    slot = x_rows[:, FEATS : FEATS + 1].astype(f32).astype(i32)
    return jnp.where(iota((x_rows.shape[0], LANES), 1) == slot - 1, 1.0, 0.0).astype(bf16)


def pack_kernel(count_ref, band_ref, slot_ref, inst_ref, raw_ref, out_ref):
    rows = band_ref.shape[1]
    slots = out_ref.shape[0]
    bands = slots // CAP_ROWS
    band = band_ref[...]
    live = iota((1, rows), 1) < count_ref[0]
    dest = jnp.where(live, band, -1)
    named = iota((bands, rows), 0) == dest
    hot = jnp.where(named, 1.0, 0.0).astype(bf16)
    earlier = jnp.where(iota((rows, rows), 0) < iota((rows, rows), 1), 1.0, 0.0).astype(bf16)
    before = dot_nn(hot, earlier)
    rank = jnp.sum(jnp.where(named, before, 0.0), axis=0, keepdims=True).astype(i32)
    position = jnp.where(live, band * CAP_ROWS + rank, -1)
    pick = jnp.where(iota((slots, rows), 0) == position, 1.0, 0.0).astype(bf16)
    part = iota((LANES - FEATS, rows), 0)
    meta = jnp.where(
        part == 0,
        (slot_ref[...] + 1).astype(f32),
        jnp.where(part == 1, inst_ref[...].astype(f32), 0.0),
    ).astype(bf16)
    payload = jnp.concatenate([raw_ref[...], meta], axis=0)
    out_ref[...] = dot_nt(pick, payload).astype(bf16)


def cross_kernel(
    x_ref,
    wk_ref,
    wv_ref,
    table_ref,
    query_ref,
    lines_ref,
    tok_ref,
    cot_ref,
    zq_ref,
    zk_ref,
    zv_ref,
    resid_ref,
    normed_ref,
    key_ref,
    val_ref,
    slope_ref,
    qs_ref,
    tanh_ref,
    prob_ref,
    ntanh_ref,
    nprob_ref,
    lines_out,
    cot_out,
    zq_out,
    zk_out,
    zv_out,
    both_s,
    query_s,
    tok_s,
    hot_s,
    inst_s,
    weight_s,
    sems,
):
    slots = x_ref.shape[0]
    feats, width = wk_ref.shape
    kinds = table_ref.shape[0]
    toks = tok_ref.shape[0]
    first = LANES + kinds
    moves = [
        pltpu.make_async_copy(src, dst, sems.at[k])
        for k, (src, dst) in enumerate(
            (
                (wk_ref, both_s.at[:feats, :width]),
                (wv_ref, both_s.at[:feats, width:]),
                (table_ref, both_s.at[LANES:first, width:]),
                (query_ref, query_s),
                (lines_ref, lines_out),
                (tok_ref, tok_s),
                (zq_ref, zq_out),
                (zk_ref, zk_out),
                (zv_ref, zv_out),
                (cot_ref, cot_out),
            )
        )
    ]
    for move in moves:
        move.start()
    both_s[feats:LANES, :] = jnp.zeros((LANES - feats, 2 * width), bf16)
    both_s[LANES:first, :width] = jnp.zeros((kinds, width), bf16)
    both_s[first:, :] = jnp.zeros((LANES - kinds, 2 * width), bf16)
    head_sum = head_sum_matrix(width)
    head_spread = head_spread_matrix(width)
    for start in range(0, slots, ROW_BLOCK):
        span = pl.ds(start, ROW_BLOCK)
        x = x_ref[span, :]
        hot_s[span, :] = token_hot(x)
        inst = x[:, FEATS + 1 : FEATS + 2].astype(f32).astype(i32)
        inst_s[span, :] = jnp.where(
            iota((ROW_BLOCK, LANES), 1) == inst, 1.0, 0.0
        ).astype(bf16)
    for move in moves[:4]:
        move.wait()
    w_both = both_s[...]
    query = query_s[...]
    total = jnp.zeros((toks, LANES), f32)
    for start in range(0, slots, ROW_BLOCK):
        span = pl.ds(start, ROW_BLOCK)
        hot = hot_s[span, :]
        encoded = dot_nn(jnp.concatenate([x_ref[span, :], inst_s[span, :]], axis=1), w_both)
        keys = encoded[:, :width].astype(bf16)
        key_ref[span, :] = keys
        pre = encoded[:, width:]
        sigma = 1.0 / (1.0 + jnp.exp(-pre))
        val_ref[span, :] = (pre * sigma).astype(bf16)
        slope_ref[span, :] = (sigma * (1.0 + pre * (1.0 - sigma))).astype(bf16)
        q_slot = dot_nn(hot, query).astype(bf16)
        qs_ref[span, :] = q_slot
        t = jnp.tanh(dot_nn(q_slot * keys, head_sum) * (score_scale / logit_cap))
        tanh_ref[span, :] = t
        weight = jnp.exp(logit_cap * t)
        weight_s[span, :] = weight
        total = total + fine_tn(hot, weight)
    for move in moves[4:6]:
        move.wait()
    null_key = lines_out[0:1, :]
    null_val = lines_out[1:2, :]
    gain = lines_out[2:3, :]
    null_t = jnp.tanh(
        fine_nn_left(query.astype(f32) * null_key, head_sum)
        * (score_scale / logit_cap)
    )
    null_weight = jnp.exp(logit_cap * null_t)
    share = 1.0 / (total + null_weight)
    null_prob = null_weight * share
    ntanh_ref[...] = null_t
    nprob_ref[...] = null_prob
    gathered = dot_nn(null_prob.astype(bf16), head_spread) * null_val
    for start in range(0, slots, ROW_BLOCK):
        span = pl.ds(start, ROW_BLOCK)
        hot = hot_s[span, :]
        prob = weight_s[span, :] * fine_nn(doubled(hot), share)
        prob_ref[span, :] = prob
        spread = dot_nn(prob.astype(bf16), head_spread).astype(bf16)
        gathered = gathered + dot_tn(hot, spread * val_ref[span, :])
    resid = (tok_s[...].astype(f32) + gathered).astype(bf16)
    resid_ref[...] = resid
    resid_f = resid.astype(f32)
    inverse = lax.rsqrt(jnp.mean(resid_f * resid_f, axis=1, keepdims=True) + norm_eps)
    normed_ref[...] = (resid_f * inverse * gain).astype(bf16)
    for move in moves[6:]:
        move.wait()


def zonal_kernel(
    me_ref,
    normed_ref,
    att_ref,
    zq_ref,
    zk_ref,
    zv_ref,
    resid_ref,
    cot_ref,
    lines_ref,
    dres_ref,
    zq_s,
    zk_s,
    zkt_s,
    zv_s,
    att_s,
    norm_s,
    dq_s,
    dk_s,
    dv_s,
    top_s,
    prob_s,
    col_s,
):
    whole, width = normed_ref.shape
    own = resid_ref.shape[0]
    sectors = whole // own
    pairs = width // LANES
    me = me_ref[0]
    for k in range(sectors):
        src = pl.multiple_of(lax.rem(me + k, sectors) * own, own)
        norm_s[k * own : (k + 1) * own, :] = normed_ref[pl.ds(src, own), :]
        part = att_ref[pl.ds(src, own), :]
        for p in range(pairs):
            att_s[p, k * own : (k + 1) * own, :] = part[:, p * LANES : (p + 1) * LANES]
    normed = norm_s[...]
    for ref, out in ((zq_ref, zq_s), (zk_ref, zk_s), (zv_ref, zv_s)):
        proj = dot_nn(normed, ref[...])
        for p in range(pairs):
            piece = proj[:, p * LANES : (p + 1) * LANES]
            out[p] = piece.astype(bf16)
            if out is zk_s:
                zkt_s[p] = piece.T.astype(bf16)
    lane_head = iota((whole, LANES), 1) // HEAD_DIM
    low_half = iota((own, LANES), 1) < HEAD_DIM

    def scores(p):
        keys = zk_s[p]
        vals = zv_s[p]
        for head in range(2):
            rows = slice(head * own, (head + 1) * own)
            qm = jnp.where(lane_head == head, zq_s[p], jnp.zeros((), bf16))
            am = jnp.where(lane_head == head, att_s[p], jnp.zeros((), bf16))
            t = jnp.tanh(dot_nt(keys, qm) * (score_scale / logit_cap))
            zdp = dot_nt(vals, am)
            weight = jnp.exp(logit_cap * t)
            share = 1.0 / jnp.sum(weight, axis=0, keepdims=True)
            inner = jnp.sum(weight * zdp, axis=0, keepdims=True) * share
            scaled = share * score_scale
            top = (
                weight[:own] * scaled * (zdp[:own] - inner) * (1.0 - t[:own] * t[:own])
            ).astype(bf16)
            rest = (
                weight[own:, :own]
                * scaled[:, :own]
                * (zdp[own:, :own] - inner[:, :own])
                * (1.0 - t[own:, :own] * t[own:, :own])
            ).astype(bf16)
            top_s[p, rows, :] = top
            prob_s[p, rows, :] = (weight[:own] * share).astype(bf16)
            col_s[p, :own, rows] = top[:, :own]
            col_s[p, own:, rows] = rest

    def gradients(p):
        dk = dot_nn(top_s[p], zq_s[p])
        dk_s[p] = jnp.where(low_half, dk[:own], dk[own:]).astype(bf16)
        dv = dot_nn(prob_s[p], att_s[p])
        dv_s[p] = jnp.where(low_half, dv[:own], dv[own:]).astype(bf16)
        dq = dot_nn(zkt_s[p], col_s[p])
        dq_s[p, :HEAD_DIM, :] = dq[:HEAD_DIM, :own]
        dq_s[p, HEAD_DIM:, :] = dq[HEAD_DIM:, own:]

    for p in range(pairs):
        scores(p)
    for p in range(pairs):
        gradients(p)
    d_normed = jnp.zeros((own, width), f32)
    for p in range(pairs):
        cols = slice(p * LANES, (p + 1) * LANES)
        d_normed = d_normed + dot_nt(dq_s[p].T.astype(bf16), zq_ref[:, cols])
        d_normed = d_normed + dot_nt(dk_s[p], zk_ref[:, cols])
        d_normed = d_normed + dot_nt(dv_s[p], zv_ref[:, cols])
    resid_f = resid_ref[...].astype(f32)
    inverse = lax.rsqrt(jnp.mean(resid_f * resid_f, axis=1, keepdims=True) + norm_eps)
    gained = lines_ref[2:3, :] * d_normed
    dres_ref[...] = (
        cot_ref[...].astype(f32)
        + inverse * gained
        - resid_f * (inverse * inverse * inverse) * jnp.mean(resid_f * gained, axis=1, keepdims=True)
    ).astype(bf16)


def back_kernel(
    x_ref,
    dres_ref,
    lines_ref,
    val_ref,
    slope_ref,
    qs_ref,
    tanh_ref,
    prob_ref,
    ntanh_ref,
    nprob_ref,
    grad_ref,
    draw_ref,
    nraw_ref,
    ds_s,
    dp_s,
    hot_s,
):
    slots = x_ref.shape[0]
    toks, width = dres_ref.shape
    head_sum = head_sum_matrix(width)
    head_spread = head_spread_matrix(width)
    d_resid = dres_ref[...]
    null_prob = nprob_ref[...]
    null_t = ntanh_ref[...]
    null_dp = fine_nn_left(d_resid.astype(f32) * lines_ref[1:2, :], head_sum)
    inner = null_prob * null_dp
    for start in range(0, slots, ROW_BLOCK):
        span = pl.ds(start, ROW_BLOCK)
        hot = token_hot(x_ref[span, :])
        hot_s[span, :] = hot
        d_slot = dot_nn(hot, d_resid).astype(bf16)
        ds_s[span, :] = d_slot
        dp = dot_nn(d_slot * val_ref[span, :], head_sum)
        dp_s[span, :] = dp
        inner = inner + fine_tn(hot, prob_ref[span, :] * dp)
    nraw_ref[...] = null_prob * (null_dp - inner) * (1.0 - null_t * null_t) * score_scale
    grads = jnp.zeros((LANES, 2 * width), f32)
    for start in range(0, slots, ROW_BLOCK):
        span = pl.ds(start, ROW_BLOCK)
        prob = prob_ref[span, :]
        t = tanh_ref[span, :]
        d_raw = (
            prob
            * (dp_s[span, :] - fine_nn(doubled(hot_s[span, :]), inner))
            * (1.0 - t * t)
            * score_scale
        ).astype(bf16)
        draw_ref[span, :] = d_raw
        d_raw_wide = dot_nn(d_raw, head_spread).astype(bf16)
        prob_wide = dot_nn(prob.astype(bf16), head_spread).astype(bf16)
        d_keys = d_raw_wide * qs_ref[span, :]
        d_pre = (prob_wide * ds_s[span, :]) * slope_ref[span, :]
        grads = grads + dot_tn(x_ref[span, :], jnp.concatenate([d_keys, d_pre], axis=1))
    blocks = 2 * width // LANES
    for b in range(blocks):
        grad_ref[b * FEATS : (b + 1) * FEATS, :] = grads[
            :FEATS, b * LANES : (b + 1) * LANES
        ].astype(bf16)
    spare = grad_ref.shape[0] - blocks * FEATS
    grad_ref[blocks * FEATS :, :] = jnp.zeros((spare, LANES), bf16)


def token_kernel(x_ref, dres_ref, lines_ref, key_ref, draw_ref, nraw_ref, wq_ref, dtok_ref):
    slots = x_ref.shape[0]
    head_spread = head_spread_matrix(dres_ref.shape[1])
    d_query = fine_nn_left(nraw_ref[...], head_spread) * lines_ref[0:1, :]
    for start in range(0, slots, ROW_BLOCK):
        span = pl.ds(start, ROW_BLOCK)
        d_raw_wide = dot_nn(draw_ref[span, :], head_spread).astype(bf16)
        hot = token_hot(x_ref[span, :])
        d_query = d_query + dot_tn(hot, d_raw_wide * key_ref[span, :])
    d_tok = dres_ref[...].astype(f32) + dot_nt(d_query.astype(bf16), wq_ref[...])
    dtok_ref[...] = d_tok.astype(bf16)


def in_vmem(value):
    return pltpu.with_memory_space_constraint(value, pltpu.VMEM)


def unpack_kernel(scale, parts_ref, key_ref, value_ref):
    width = key_ref.shape[1]
    pieces = width // LANES
    for g, out in enumerate((key_ref, value_ref)):
        for b in range(pieces):
            start = (g * pieces + b) * FEATS
            rows = parts_ref[start : start + FEATS, :].astype(f32)
            out[:, b * LANES : (b + 1) * LANES] = rows * scale


def in_hbm(value):
    return pltpu.with_memory_space_constraint(value, pltpu.HBM)


def whole_call(
    kernel, name, out_shape, args, scalars=0, fetched=0, far=0, scratch=(), scoped=16
):
    smem = pl.BlockSpec(memory_space=pltpu.SMEM)
    vmem = pl.BlockSpec(memory_space=pltpu.VMEM)
    hbm = pl.BlockSpec(memory_space=pltpu.HBM)
    several = isinstance(out_shape, (list, tuple))
    first, last = scalars + fetched, len(args) - far
    args = (
        tuple(args[:scalars])
        + tuple(in_hbm(a) for a in args[scalars:first])
        + tuple(in_vmem(a) for a in args[first:last])
        + tuple(in_hbm(a) for a in args[last:])
    )
    return pl.pallas_call(
        kernel,
        name=name,
        out_shape=out_shape,
        in_specs=[smem] * scalars + [vmem] * (last - scalars) + [hbm] * far,
        out_specs=[vmem] * len(out_shape) if several else vmem,
        scratch_shapes=list(scratch),
        compiler_params=pltpu.CompilerParams(vmem_limit_bytes=scoped * 1024 * 1024),
    )(*args)


def plain(rows, cols, dtype):
    return jax.ShapeDtypeStruct((rows, cols), dtype)


def shaped(rows, cols, dtype):
    return pltpu.VMEM((rows, cols), dtype)


def pack(obs_count, obs_band, obs_slot, obs_inst, raw_obs, bands):
    rows = raw_obs.shape[0]
    return whole_call(
        pack_kernel,
        "pack",
        plain(bands * CAP_ROWS, LANES, bf16),
        (
            obs_count,
            obs_band.reshape(1, rows),
            obs_slot.reshape(1, rows),
            obs_inst.reshape(1, rows),
            raw_obs.T,
        ),
        scalars=1,
        fetched=4,
    )


def cross_forward(x, w_key, w_val, table, query, lines, tok, cot, zq, zk, zv):
    slots = x.shape[0]
    toks, width = tok.shape
    big = shaped(slots, width, bf16)
    small = shaped(slots, LANES, f32)
    null = shaped(toks, LANES, f32)
    row = shaped(toks, width, bf16)
    square = shaped(*zq.shape, bf16)
    far = (w_key, w_val, table, query, lines, tok, cot, zq, zk, zv)
    return whole_call(
        cross_kernel,
        "cross_forward",
        [row, row, big, big, big, big, small, small, null, null]
        + [shaped(*lines.shape, f32), row, square, square, square],
        (x,) + far,
        far=len(far),
        scratch=(
            pltpu.VMEM((2 * LANES, 2 * width), bf16),
            pltpu.VMEM((toks, width), bf16),
            pltpu.VMEM((toks, width), bf16),
            pltpu.VMEM((slots, LANES), bf16),
            pltpu.VMEM((slots, LANES), bf16),
            pltpu.VMEM((slots, LANES), f32),
            pltpu.SemaphoreType.DMA((len(far),)),
        ),
    )


def zonal(me, normed_all, att_all, zq, zk, zv, resid, cot, lines):
    own, width = resid.shape
    whole = normed_all.shape[0]
    pairs = width // LANES
    rows = pltpu.VMEM((pairs, whole, LANES), bf16)
    return whole_call(
        zonal_kernel,
        "zonal",
        shaped(own, width, bf16),
        (me, normed_all, att_all, zq, zk, zv, resid, cot, lines),
        scalars=1,
        scratch=(
            rows,
            rows,
            pltpu.VMEM((pairs, LANES, whole), bf16),
            rows,
            rows,
            pltpu.VMEM((whole, width), bf16),
            pltpu.VMEM((pairs, LANES, own), f32),
            pltpu.VMEM((pairs, own, LANES), bf16),
            pltpu.VMEM((pairs, own, LANES), bf16),
            pltpu.VMEM((pairs, 2 * own, whole), bf16),
            pltpu.VMEM((pairs, 2 * own, whole), bf16),
            pltpu.VMEM((pairs, whole, 2 * own), bf16),
        ),
    )


def cross_backward(x, d_resid, lines, saved):
    slots = x.shape[0]
    toks, width = d_resid.shape
    return whole_call(
        back_kernel,
        "cross_backward",
        [
            shaped(PLANE * CHUNK, LANES, bf16),
            shaped(slots, LANES, bf16),
            shaped(toks, LANES, f32),
        ],
        (x, d_resid, lines) + tuple(saved),
        scratch=(
            pltpu.VMEM((slots, width), bf16),
            pltpu.VMEM((slots, LANES), f32),
            pltpu.VMEM((slots, LANES), bf16),
        ),
    )


def token_gradient(x, d_resid, lines, keys, d_raw, null_raw, w_query):
    return whole_call(
        token_kernel,
        "token_gradient",
        plain(*d_resid.shape, bf16),
        (x, d_resid, lines, keys, d_raw, null_raw, w_query),
    )


def unpack(parts, width, scale):
    out = plain(FEATS, width, f32)
    return whole_call(
        functools.partial(unpack_kernel, scale), "unpack", [out, out], (parts,)
    )


def sum_everywhere(rows):
    plane = [list(range(z * PLANE, (z + 1) * PLANE)) for z in range(DEPTH)]
    lats = PLANE // 4
    column = [[z * lats + k for z in range(DEPTH)] for k in range(lats)]

    def swap(parts, axes, groups):
        return lax.all_to_all(
            parts, axes, split_axis=0, concat_axis=0, tiled=True, axis_index_groups=groups
        )

    def total(parts):
        return jnp.sum(parts.astype(f32), axis=0)

    parts = swap(rows.reshape(PLANE, CHUNK, LANES), ("lat", "lon"), plane)
    mine = total(parts).astype(bf16)
    parts = swap(jnp.broadcast_to(mine, (DEPTH, CHUNK, LANES)), "lat", column)
    mine = total(parts).astype(bf16)
    parts = swap(jnp.broadcast_to(mine, (PLANE, CHUNK, LANES)), ("lat", "lon"), plane)
    return parts.reshape(PLANE * CHUNK, LANES)


def on_device(
    tokens,
    cotangent,
    raw_obs,
    obs_band,
    obs_slot,
    obs_inst,
    obs_count,
    w_key_obs,
    w_val_obs,
    inst_table,
    null_key,
    null_val,
    w_query,
    norm_gain,
    zonal_query,
    zonal_key,
    zonal_value,
    zonal_out,
):
    tok_rows, width = tokens.shape[1:]
    bands = lax.axis_size("lat")
    devices = bands * lax.axis_size("lon")
    obs_total = raw_obs.shape[0] * devices
    tok = tokens.reshape(tok_rows, width)
    cot = cotangent.reshape(tok_rows, width)
    lines = jnp.stack([null_key.astype(f32), null_val.astype(f32), norm_gain])
    lines = jnp.concatenate([lines, jnp.zeros((5, width), f32)], axis=0)
    packed = pack(obs_count, obs_band, obs_slot, obs_inst, raw_obs, bands)
    received = lax.all_to_all(
        packed.reshape(bands, CAP_ROWS, LANES), "lat", split_axis=0, concat_axis=0, tiled=True
    ).reshape(bands * CAP_ROWS, LANES)
    query = jnp.dot(tok, w_query, preferred_element_type=f32).astype(bf16)
    d_att = dot_nt(cot, zonal_out).astype(bf16)
    att_all = lax.all_gather(d_att, "lon", axis=0, tiled=True)
    resid, normed, keys, *saved, lines, cot, zq, zk, zv = cross_forward(
        received,
        w_key_obs,
        w_val_obs,
        inst_table,
        query,
        lines,
        tok,
        cot,
        zonal_query,
        zonal_key,
        zonal_value,
    )
    normed_all = lax.all_gather(normed, "lon", axis=0, tiled=True)
    me = lax.axis_index("lon").astype(i32).reshape(1)
    d_resid = zonal(me, normed_all, att_all, zq, zk, zv, resid, cot, lines)
    grads, d_raw, null_raw = cross_backward(received, d_resid, lines, saved)
    d_tok = token_gradient(received, d_resid, lines, keys, d_raw, null_raw, w_query)
    key_grad, value_grad = unpack(sum_everywhere(grads), width, 1.0 / math.sqrt(obs_total))
    return d_tok.reshape(1, tok_rows, width), key_grad, value_grad


def solution(mesh):
    return jax.shard_map(
        on_device,
        mesh=mesh,
        in_specs=(
            P("lat", "lon", None),
            P("lat", "lon", None),
            P(("lat", "lon"), None),
            P(("lat", "lon"), None),
            P(("lat", "lon")),
            P(("lat", "lon")),
            P(("lat", "lon")),
            P(),
            P(),
            P(),
            P(),
            P(),
            P(),
            P(),
            P(),
            P(),
            P(),
            P(),
        ),
        out_specs=(P("lat", "lon", None), P(), P()),
        check_vma=False,
    )
```

```python
import functools
import math

import jax
import jax.numpy as jnp
from jax import lax
from jax.experimental import pallas as pl
from jax.experimental.pallas import tpu as pltpu
from jax.sharding import PartitionSpec as P

HEAD_DIM = 64
CAP_ROWS = 8
LANES = 128
FEATS = 64

logit_cap = 6.0
norm_eps = 1e-06
score_scale = 1.0 / math.sqrt(HEAD_DIM)
LOG2E = math.log2(math.e)

bf16 = jnp.bfloat16
f32 = jnp.float32
i32 = jnp.int32

PLANE = 32
DEPTH = 16
CHUNK = 24
ROW_BLOCK = 1024


def iota(shape, dim):
    return lax.broadcasted_iota(i32, shape, dim)


def dot_nn(a, b):
    return lax.dot_general(a, b, (((1,), (0,)), ((), ())), preferred_element_type=f32)


def dot_nt(a, b):
    return lax.dot_general(a, b, (((1,), (1,)), ((), ())), preferred_element_type=f32)


def dot_tn(a, b):
    return lax.dot_general(a, b, (((0,), (0,)), ((), ())), preferred_element_type=f32)


def halves(value):
    high = value.astype(bf16)
    return high, (value - high.astype(f32)).astype(bf16)


def fine_nn(twice, value):
    return dot_nn(twice, jnp.concatenate(halves(value), axis=0))


def fine_tn(a, value):
    both = dot_tn(a, jnp.concatenate(halves(value), axis=1))
    return both[:, : value.shape[1]] + both[:, value.shape[1] :]


def fine_nn_left(value, b):
    high, low = halves(value)
    return dot_nn(high, b) + dot_nn(low, b)


def doubled(hot):
    return jnp.concatenate([hot, hot], axis=1)


def head_sum_matrix(width):
    return jnp.where(
        iota((width, LANES), 0) // HEAD_DIM == iota((width, LANES), 1), 1.0, 0.0
    ).astype(bf16)


def head_spread_matrix(width):
    return jnp.where(
        iota((LANES, width), 1) // HEAD_DIM == iota((LANES, width), 0), 1.0, 0.0
    ).astype(bf16)


def token_hot(x_rows):
    slot = x_rows[:, FEATS : FEATS + 1].astype(f32).astype(i32)
    return jnp.where(iota((x_rows.shape[0], LANES), 1) == slot - 1, 1.0, 0.0).astype(bf16)


def pack_kernel(
    count_ref,
    band_hbm,
    slot_hbm,
    inst_hbm,
    raw_hbm,
    out_hbm,
    band_ref,
    slot_ref,
    inst_ref,
    raw_ref,
    out_ref,
    in_sems,
    out_sems,
):
    moves = [
        pltpu.make_async_copy(src, dst, in_sems.at[k])
        for k, (src, dst) in enumerate(
            (
                (band_hbm, band_ref),
                (raw_hbm, raw_ref),
                (slot_hbm, slot_ref),
                (inst_hbm, inst_ref),
            )
        )
    ]
    for move in moves:
        move.start()
    rows = band_ref.shape[1]
    slots = out_ref.shape[0]
    bands = slots // CAP_ROWS
    earlier = jnp.where(iota((rows, rows), 0) < iota((rows, rows), 1), 1.0, 0.0).astype(bf16)
    moves[0].wait()
    band = band_ref[...]
    live = iota((1, rows), 1) < count_ref[0]
    dest = jnp.where(live, band, -1)
    named = iota((bands, rows), 0) == dest
    hot = jnp.where(named, 1.0, 0.0).astype(bf16)
    before = dot_nn(hot, earlier)
    rank = jnp.sum(jnp.where(named, before, 0.0), axis=0, keepdims=True).astype(i32)
    position = jnp.where(live, band * CAP_ROWS + rank, -1)
    for move in moves[1:]:
        move.wait()
    part = iota((LANES - FEATS, rows), 0)
    meta = jnp.where(
        part == 0,
        (slot_ref[...] + 1).astype(f32),
        jnp.where(part == 1, inst_ref[...].astype(f32), 0.0),
    ).astype(bf16)
    payload = jnp.concatenate([raw_ref[...], meta], axis=0)
    step = slots // out_sems.shape[0]
    leaving = []
    for k in range(out_sems.shape[0]):
        span = pl.ds(k * step, step)
        pick = jnp.where(iota((step, rows), 0) + k * step == position, 1.0, 0.0).astype(bf16)
        out_ref[span, :] = dot_nt(pick, payload).astype(bf16)
        leaving.append(
            pltpu.make_async_copy(out_ref.at[span], out_hbm.at[span], out_sems.at[k])
        )
        leaving[-1].start()
    for move in leaving:
        move.wait()


def cross_kernel(
    x_ref,
    wk_ref,
    wv_ref,
    table_ref,
    query_ref,
    lines_ref,
    tok_ref,
    cot_ref,
    zq_ref,
    zk_ref,
    zv_ref,
    resid_ref,
    normed_ref,
    key_ref,
    val_ref,
    slope_ref,
    qs_ref,
    tanh_ref,
    prob_ref,
    ntanh_ref,
    nprob_ref,
    lines_out,
    cot_out,
    zq_out,
    zk_out,
    zv_out,
    both_s,
    query_s,
    tok_s,
    keys_s,
    hot_s,
    inst_s,
    weight_s,
    sems,
    key_sem,
):
    slots = x_ref.shape[0]
    feats, width = wk_ref.shape
    kinds = table_ref.shape[0]
    toks = tok_ref.shape[0]
    first = LANES + kinds
    moves = [
        pltpu.make_async_copy(src, dst, sems.at[k])
        for k, (src, dst) in enumerate(
            (
                (wk_ref, both_s.at[:feats, :width]),
                (wv_ref, both_s.at[:feats, width:]),
                (table_ref, both_s.at[LANES:first, width:]),
                (query_ref, query_s),
                (lines_ref, lines_out),
                (tok_ref, tok_s),
                (zq_ref, zq_out),
                (zk_ref, zk_out),
                (zv_ref, zv_out),
                (cot_ref, cot_out),
            )
        )
    ]
    for move in moves[:6]:
        move.start()
    both_s[feats:LANES, :] = jnp.zeros((LANES - feats, 2 * width), bf16)
    both_s[LANES:first, :width] = jnp.zeros((kinds, width), bf16)
    both_s[first:, :] = jnp.zeros((LANES - kinds, 2 * width), bf16)
    head_sum = head_sum_matrix(width)
    head_spread = head_spread_matrix(width)
    for start in range(0, slots, ROW_BLOCK):
        span = pl.ds(start, ROW_BLOCK)
        x = x_ref[span, :]
        hot_s[span, :] = token_hot(x)
        inst = x[:, FEATS + 1 : FEATS + 2].astype(f32).astype(i32)
        inst_s[span, :] = jnp.where(
            iota((ROW_BLOCK, LANES), 1) == inst, 1.0, 0.0
        ).astype(bf16)
    for move in moves[:4]:
        move.wait()
    for move in moves[6:]:
        move.start()
    w_both = both_s[...]
    query = query_s[...]
    total = jnp.zeros((toks, LANES), f32)
    for start in range(0, slots, ROW_BLOCK):
        span = pl.ds(start, ROW_BLOCK)
        hot = hot_s[span, :]
        encoded = dot_nn(jnp.concatenate([x_ref[span, :], inst_s[span, :]], axis=1), w_both)
        keys = encoded[:, :width].astype(bf16)
        keys_s[span, :] = keys
        pre = encoded[:, width:]
        sigma = 0.5 + 0.5 * jnp.tanh(0.5 * pre)
        val_ref[span, :] = (pre * sigma).astype(bf16)
        slope_ref[span, :] = (sigma * (1.0 + pre * (1.0 - sigma))).astype(bf16)
        q_slot = dot_nn(hot, query).astype(bf16)
        qs_ref[span, :] = q_slot
        t = jnp.tanh(dot_nn(q_slot * keys, head_sum) * (score_scale / logit_cap))
        tanh_ref[span, :] = t
        weight = jnp.exp(logit_cap * t)
        weight_s[span, :] = weight
        total = total + fine_tn(hot, weight)
    away = pltpu.make_async_copy(keys_s, key_ref, key_sem)
    away.start()
    for move in moves[4:6]:
        move.wait()
    null_key = lines_out[0:1, :]
    null_val = lines_out[1:2, :]
    gain = lines_out[2:3, :]
    null_t = jnp.tanh(
        fine_nn_left(query.astype(f32) * null_key, head_sum)
        * (score_scale / logit_cap)
    )
    null_weight = jnp.exp(logit_cap * null_t)
    share = 1.0 / (total + null_weight)
    null_prob = null_weight * share
    ntanh_ref[...] = null_t
    nprob_ref[...] = null_prob
    gathered = dot_nn(null_prob.astype(bf16), head_spread) * null_val
    for start in range(0, slots, ROW_BLOCK):
        span = pl.ds(start, ROW_BLOCK)
        hot = hot_s[span, :]
        prob = weight_s[span, :] * fine_nn(doubled(hot), share)
        prob_ref[span, :] = prob
        spread = dot_nn(prob.astype(bf16), head_spread).astype(bf16)
        gathered = gathered + dot_tn(hot, spread * val_ref[span, :])
    resid = (tok_s[...].astype(f32) + gathered).astype(bf16)
    resid_ref[...] = resid
    resid_f = resid.astype(f32)
    inverse = lax.rsqrt(jnp.mean(resid_f * resid_f, axis=1, keepdims=True) + norm_eps)
    normed_ref[...] = (resid_f * inverse * gain).astype(bf16)
    for move in moves[6:]:
        move.wait()
    away.wait()


def zonal_kernel(
    me_ref,
    normed_ref,
    att_ref,
    zq_ref,
    zk_ref,
    zv_ref,
    resid_ref,
    cot_ref,
    lines_ref,
    dres_ref,
    zq_s,
    zk_s,
    zkt_s,
    zv_s,
    att_s,
    norm_s,
    dq_s,
    dk_s,
    dv_s,
    top_s,
    prob_s,
    col_s,
):
    whole, width = normed_ref.shape
    own = resid_ref.shape[0]
    sectors = whole // own
    pairs = width // LANES
    me = me_ref[0]
    for k in range(sectors):
        src = pl.multiple_of(lax.rem(me + k, sectors) * own, own)
        norm_s[k * own : (k + 1) * own, :] = normed_ref[pl.ds(src, own), :]
        part = att_ref[pl.ds(src, own), :]
        for p in range(pairs):
            att_s[p, k * own : (k + 1) * own, :] = part[:, p * LANES : (p + 1) * LANES]
    normed = norm_s[...]
    for ref, out in ((zq_ref, zq_s), (zk_ref, zk_s), (zv_ref, zv_s)):
        proj = dot_nn(normed, ref[...])
        for p in range(pairs):
            piece = proj[:, p * LANES : (p + 1) * LANES]
            out[p] = piece.astype(bf16)
            if out is zk_s:
                zkt_s[p] = piece.astype(bf16).T
    lane_head = iota((whole, LANES), 1) // HEAD_DIM
    low_half = iota((own, LANES), 1) < HEAD_DIM

    def scores(p):
        keys = zk_s[p]
        vals = zv_s[p]
        for head in range(2):
            rows = slice(head * own, (head + 1) * own)
            qm = jnp.where(lane_head == head, zq_s[p], jnp.zeros((), bf16))
            am = jnp.where(lane_head == head, att_s[p], jnp.zeros((), bf16))
            half = whole // 2
            for start in (0, half):
                cols = slice(start, start + half)
                t = jnp.tanh(dot_nt(keys, qm[cols]) * (score_scale / logit_cap))
                zdp = dot_nt(vals, am[cols])
                weight = jnp.exp2((logit_cap * LOG2E) * t)
                share = 1.0 / jnp.sum(weight, axis=0, keepdims=True)
                inner = jnp.sum(weight * zdp, axis=0, keepdims=True) * share
                t_top = t[:own]
                prob = weight[:own] * share
                top = (prob * (zdp[:own] - inner) * (1.0 - t_top * t_top)).astype(bf16)
                top_s[p, rows, cols] = top
                prob_s[p, rows, cols] = prob.astype(bf16)
                if start == 0:
                    t_rest = t[own:, :own]
                    rest = (
                        (weight[own:, :own] * share[:, :own])
                        * (zdp[own:, :own] - inner[:, :own])
                        * (1.0 - t_rest * t_rest)
                    ).astype(bf16)
                    col_s[p, :own, rows] = top[:, :own]
                    col_s[p, own:, rows] = rest

    def gradients(p):
        dk = dot_nn(top_s[p], zq_s[p])
        dk_s[p] = (jnp.where(low_half, dk[:own], dk[own:]) * score_scale).astype(bf16)
        dv = dot_nn(prob_s[p], att_s[p])
        dv_s[p] = jnp.where(low_half, dv[:own], dv[own:]).astype(bf16)
        dq = dot_nn(zkt_s[p], col_s[p])
        dq_s[p, :HEAD_DIM, :] = dq[:HEAD_DIM, :own] * score_scale
        dq_s[p, HEAD_DIM:, :] = dq[HEAD_DIM:, own:] * score_scale

    for p in range(pairs):
        scores(p)
    for p in range(pairs):
        gradients(p)
    d_zq = jnp.concatenate([dq_s[p].T.astype(bf16) for p in range(pairs)], axis=1)
    d_zk = jnp.concatenate([dk_s[p] for p in range(pairs)], axis=1)
    d_zv = jnp.concatenate([dv_s[p] for p in range(pairs)], axis=1)
    d_normed = (
        dot_nt(d_zq, zq_ref[...]) + dot_nt(d_zk, zk_ref[...]) + dot_nt(d_zv, zv_ref[...])
    )
    resid_f = resid_ref[...].astype(f32)
    inverse = lax.rsqrt(jnp.mean(resid_f * resid_f, axis=1, keepdims=True) + norm_eps)
    gained = lines_ref[2:3, :] * d_normed
    dres_ref[...] = (
        cot_ref[...].astype(f32)
        + inverse * gained
        - resid_f * (inverse * inverse * inverse) * jnp.mean(resid_f * gained, axis=1, keepdims=True)
    ).astype(bf16)


def back_kernel(
    x_ref,
    dres_ref,
    lines_ref,
    val_ref,
    slope_ref,
    qs_ref,
    tanh_ref,
    prob_ref,
    ntanh_ref,
    nprob_ref,
    grad_ref,
    draw_ref,
    nraw_ref,
    ds_s,
    dp_s,
    hot_s,
):
    slots = x_ref.shape[0]
    toks, width = dres_ref.shape
    head_sum = head_sum_matrix(width)
    head_spread = head_spread_matrix(width)
    d_resid = dres_ref[...]
    null_prob = nprob_ref[...]
    null_t = ntanh_ref[...]
    null_dp = fine_nn_left(d_resid.astype(f32) * lines_ref[1:2, :], head_sum)
    inner = null_prob * null_dp
    for start in range(0, slots, ROW_BLOCK):
        span = pl.ds(start, ROW_BLOCK)
        hot = token_hot(x_ref[span, :])
        hot_s[span, :] = hot
        d_slot = dot_nn(hot, d_resid).astype(bf16)
        ds_s[span, :] = d_slot
        dp = dot_nn(d_slot * val_ref[span, :], head_sum)
        dp_s[span, :] = dp
        inner = inner + fine_tn(hot, prob_ref[span, :] * dp)
    nraw_ref[...] = null_prob * (null_dp - inner) * (1.0 - null_t * null_t) * score_scale
    grads = jnp.zeros((LANES, 2 * width), f32)
    for start in range(0, slots, ROW_BLOCK):
        span = pl.ds(start, ROW_BLOCK)
        prob = prob_ref[span, :]
        t = tanh_ref[span, :]
        d_raw = (
            prob
            * (dp_s[span, :] - fine_nn(doubled(hot_s[span, :]), inner))
            * (1.0 - t * t)
            * score_scale
        ).astype(bf16)
        draw_ref[span, :] = d_raw
        d_raw_wide = dot_nn(d_raw, head_spread).astype(bf16)
        prob_wide = dot_nn(prob.astype(bf16), head_spread).astype(bf16)
        d_keys = d_raw_wide * qs_ref[span, :]
        d_pre = (prob_wide * ds_s[span, :]) * slope_ref[span, :]
        grads = grads + dot_tn(x_ref[span, :], jnp.concatenate([d_keys, d_pre], axis=1))
    blocks = 2 * width // LANES
    for b in range(blocks):
        grad_ref[b * FEATS : (b + 1) * FEATS, :] = grads[
            :FEATS, b * LANES : (b + 1) * LANES
        ].astype(bf16)
    spare = grad_ref.shape[0] - blocks * FEATS
    grad_ref[blocks * FEATS :, :] = jnp.zeros((spare, LANES), bf16)


def token_kernel(
    x_ref,
    dres_ref,
    lines_ref,
    draw_ref,
    nraw_ref,
    key_ref,
    wq_ref,
    dtok_ref,
    keys_s,
    wq_s,
    sems,
):
    slots = x_ref.shape[0]
    keys_move = pltpu.make_async_copy(key_ref, keys_s, sems.at[0])
    wq_move = pltpu.make_async_copy(wq_ref, wq_s, sems.at[1])
    keys_move.start()
    wq_move.start()
    head_spread = head_spread_matrix(dres_ref.shape[1])
    d_query = fine_nn_left(nraw_ref[...], head_spread) * lines_ref[0:1, :]
    keys_move.wait()
    for start in range(0, slots, ROW_BLOCK):
        span = pl.ds(start, ROW_BLOCK)
        d_raw_wide = dot_nn(draw_ref[span, :], head_spread).astype(bf16)
        hot = token_hot(x_ref[span, :])
        d_query = d_query + dot_tn(hot, d_raw_wide * keys_s[span, :])
    wq_move.wait()
    d_tok = dres_ref[...].astype(f32) + dot_nt(d_query.astype(bf16), wq_s[...])
    dtok_ref[...] = d_tok.astype(bf16)


def in_vmem(value):
    return pltpu.with_memory_space_constraint(value, pltpu.VMEM)


def unpack_kernel(scale, parts_ref, key_ref, value_ref):
    width = key_ref.shape[1]
    pieces = width // LANES
    for g, out in enumerate((key_ref, value_ref)):
        for b in range(pieces):
            start = (g * pieces + b) * FEATS
            rows = parts_ref[start : start + FEATS, :].astype(f32)
            out[:, b * LANES : (b + 1) * LANES] = rows * scale


def in_hbm(value):
    return pltpu.with_memory_space_constraint(value, pltpu.HBM)


def whole_call(
    kernel, name, out_shape, args, scalars=0, fetched=0, far=0, away=(), scratch=(), scoped=16
):
    smem = pl.BlockSpec(memory_space=pltpu.SMEM)
    vmem = pl.BlockSpec(memory_space=pltpu.VMEM)
    hbm = pl.BlockSpec(memory_space=pltpu.HBM)
    several = isinstance(out_shape, (list, tuple))
    first, last = scalars + fetched, len(args) - far
    args = (
        tuple(args[:scalars])
        + tuple(in_hbm(a) for a in args[scalars:first])
        + tuple(in_vmem(a) for a in args[first:last])
        + tuple(in_hbm(a) for a in args[last:])
    )
    return pl.pallas_call(
        kernel,
        name=name,
        out_shape=out_shape,
        in_specs=[smem] * scalars + [vmem] * (last - scalars) + [hbm] * far,
        out_specs=[hbm if k in away else vmem for k in range(len(out_shape))]
        if several
        else vmem,
        scratch_shapes=list(scratch),
        compiler_params=pltpu.CompilerParams(vmem_limit_bytes=scoped * 1024 * 1024),
    )(*args)


def plain(rows, cols, dtype):
    return jax.ShapeDtypeStruct((rows, cols), dtype)


def shaped(rows, cols, dtype):
    return pltpu.VMEM((rows, cols), dtype)


def pack(obs_count, obs_band, obs_slot, obs_inst, raw_obs, bands):
    rows, feats = raw_obs.shape
    slots = bands * CAP_ROWS
    line = pltpu.VMEM((1, rows), i32)
    return whole_call(
        pack_kernel,
        "pack",
        [plain(slots, LANES, bf16)],
        (
            obs_count,
            obs_band.reshape(1, rows),
            obs_slot.reshape(1, rows),
            obs_inst.reshape(1, rows),
            raw_obs.T,
        ),
        scalars=1,
        far=4,
        away=(0,),
        scratch=(
            line,
            line,
            line,
            pltpu.VMEM((feats, rows), bf16),
            pltpu.VMEM((slots, LANES), bf16),
            pltpu.SemaphoreType.DMA((4,)),
            pltpu.SemaphoreType.DMA((4,)),
        ),
    )[0]


def cross_forward(x, w_key, w_val, table, query, lines, tok, cot, zq, zk, zv):
    slots = x.shape[0]
    toks, width = tok.shape
    big = shaped(slots, width, bf16)
    small = shaped(slots, LANES, f32)
    null = shaped(toks, LANES, f32)
    row = shaped(toks, width, bf16)
    square = shaped(*zq.shape, bf16)
    far = (w_key, w_val, table, query, lines, tok, cot, zq, zk, zv)
    return whole_call(
        cross_kernel,
        "cross_forward",
        [row, row, pltpu.HBM((slots, width), bf16), big, big, big, small, small, null, null]
        + [shaped(*lines.shape, f32), row, square, square, square],
        (x,) + far,
        far=len(far),
        away=(2,),
        scratch=(
            pltpu.VMEM((2 * LANES, 2 * width), bf16),
            pltpu.VMEM((toks, width), bf16),
            pltpu.VMEM((toks, width), bf16),
            pltpu.VMEM((slots, width), bf16),
            pltpu.VMEM((slots, LANES), bf16),
            pltpu.VMEM((slots, LANES), bf16),
            pltpu.VMEM((slots, LANES), f32),
            pltpu.SemaphoreType.DMA((len(far),)),
            pltpu.SemaphoreType.DMA(()),
        ),
    )


def zonal(me, normed_all, att_all, zq, zk, zv, resid, cot, lines):
    own, width = resid.shape
    whole = normed_all.shape[0]
    pairs = width // LANES
    rows = pltpu.VMEM((pairs, whole, LANES), bf16)
    return whole_call(
        zonal_kernel,
        "zonal",
        shaped(own, width, bf16),
        (me, normed_all, att_all, zq, zk, zv, resid, cot, lines),
        scalars=1,
        scratch=(
            rows,
            rows,
            pltpu.VMEM((pairs, LANES, whole), bf16),
            rows,
            rows,
            pltpu.VMEM((whole, width), bf16),
            pltpu.VMEM((pairs, LANES, own), f32),
            pltpu.VMEM((pairs, own, LANES), bf16),
            pltpu.VMEM((pairs, own, LANES), bf16),
            pltpu.VMEM((pairs, 2 * own, whole), bf16),
            pltpu.VMEM((pairs, 2 * own, whole), bf16),
            pltpu.VMEM((pairs, whole, 2 * own), bf16),
        ),
    )


def cross_backward(x, d_resid, lines, saved):
    slots = x.shape[0]
    toks, width = d_resid.shape
    return whole_call(
        back_kernel,
        "cross_backward",
        [
            shaped(PLANE * CHUNK, LANES, bf16),
            shaped(slots, LANES, bf16),
            shaped(toks, LANES, f32),
        ],
        (x, d_resid, lines) + tuple(saved),
        scratch=(
            pltpu.VMEM((slots, width), bf16),
            pltpu.VMEM((slots, LANES), f32),
            pltpu.VMEM((slots, LANES), bf16),
        ),
    )


def token_gradient(x, d_resid, lines, keys, d_raw, null_raw, w_query):
    return whole_call(
        token_kernel,
        "token_gradient",
        plain(*d_resid.shape, bf16),
        (x, d_resid, lines, d_raw, null_raw, keys, w_query),
        far=2,
        scratch=(
            pltpu.VMEM(keys.shape, bf16),
            pltpu.VMEM(w_query.shape, bf16),
            pltpu.SemaphoreType.DMA((2,)),
        ),
    )


def unpack(parts, width, scale):
    out = plain(FEATS, width, f32)
    return whole_call(
        functools.partial(unpack_kernel, scale), "unpack", [out, out], (parts,)
    )


def sum_everywhere(rows):
    plane = [list(range(z * PLANE, (z + 1) * PLANE)) for z in range(DEPTH)]
    lats = PLANE // 4
    column = [[z * lats + k for z in range(DEPTH)] for k in range(lats)]

    def swap(parts, axes, groups):
        return lax.all_to_all(
            parts, axes, split_axis=0, concat_axis=0, tiled=True, axis_index_groups=groups
        )

    def total(parts):
        return jnp.sum(parts.astype(f32), axis=0)

    parts = swap(rows.reshape(PLANE, CHUNK, LANES), ("lat", "lon"), plane)
    mine = total(parts).astype(bf16)
    parts = swap(jnp.broadcast_to(mine, (DEPTH, CHUNK, LANES)), "lat", column)
    mine = total(parts).astype(bf16)
    parts = swap(jnp.broadcast_to(mine, (PLANE, CHUNK, LANES)), ("lat", "lon"), plane)
    return parts.reshape(PLANE * CHUNK, LANES)


def on_device(
    tokens,
    cotangent,
    raw_obs,
    obs_band,
    obs_slot,
    obs_inst,
    obs_count,
    w_key_obs,
    w_val_obs,
    inst_table,
    null_key,
    null_val,
    w_query,
    norm_gain,
    zonal_query,
    zonal_key,
    zonal_value,
    zonal_out,
):
    tok_rows, width = tokens.shape[1:]
    bands = lax.axis_size("lat")
    devices = bands * lax.axis_size("lon")
    obs_total = raw_obs.shape[0] * devices
    tok = tokens.reshape(tok_rows, width)
    cot = cotangent.reshape(tok_rows, width)
    lines = jnp.stack([null_key.astype(f32), null_val.astype(f32), norm_gain])
    lines = jnp.concatenate([lines, jnp.zeros((5, width), f32)], axis=0)
    packed = pack(obs_count, obs_band, obs_slot, obs_inst, raw_obs, bands)
    received = lax.all_to_all(
        packed.reshape(bands, CAP_ROWS, LANES), "lat", split_axis=0, concat_axis=0, tiled=True
    ).reshape(bands * CAP_ROWS, LANES)
    query = jnp.dot(tok, w_query, preferred_element_type=f32).astype(bf16)
    d_att = dot_nt(cot, zonal_out).astype(bf16)
    att_all = lax.all_gather(d_att, "lon", axis=0, tiled=True)
    resid, normed, keys, *saved, lines, cot, zq, zk, zv = cross_forward(
        received,
        w_key_obs,
        w_val_obs,
        inst_table,
        query,
        lines,
        tok,
        cot,
        zonal_query,
        zonal_key,
        zonal_value,
    )
    normed_all = lax.all_gather(normed, "lon", axis=0, tiled=True)
    me = lax.axis_index("lon").astype(i32).reshape(1)
    d_resid = zonal(me, normed_all, att_all, zq, zk, zv, resid, cot, lines)
    grads, d_raw, null_raw = cross_backward(received, d_resid, lines, saved)
    d_tok = token_gradient(received, d_resid, lines, keys, d_raw, null_raw, w_query)
    key_grad, value_grad = unpack(sum_everywhere(grads), width, 1.0 / math.sqrt(obs_total))
    return d_tok.reshape(1, tok_rows, width), key_grad, value_grad


def solution(mesh):
    return jax.shard_map(
        on_device,
        mesh=mesh,
        in_specs=(
            P("lat", "lon", None),
            P("lat", "lon", None),
            P(("lat", "lon"), None),
            P(("lat", "lon"), None),
            P(("lat", "lon")),
            P(("lat", "lon")),
            P(("lat", "lon")),
            P(),
            P(),
            P(),
            P(),
            P(),
            P(),
            P(),
            P(),
            P(),
            P(),
            P(),
        ),
        out_specs=(P("lat", "lon", None), P(), P()),
        check_vma=False,
    )
```

```python
import functools
import math

import jax
import jax.numpy as jnp
from jax import lax
from jax.experimental import pallas as pl
from jax.experimental.pallas import tpu as pltpu
from jax.sharding import PartitionSpec as P

HEAD_DIM = 64
CAP_ROWS = 8
LANES = 128
FEATS = 64

logit_cap = 6.0
norm_eps = 1e-06
score_scale = 1.0 / math.sqrt(HEAD_DIM)
LOG2E = math.log2(math.e)

bf16 = jnp.bfloat16
f32 = jnp.float32
i32 = jnp.int32

PLANE = 32
DEPTH = 16
CHUNK = 24
ROW_BLOCK = 1024


def iota(shape, dim):
    return lax.broadcasted_iota(i32, shape, dim)


def dot_nn(a, b):
    return lax.dot_general(a, b, (((1,), (0,)), ((), ())), preferred_element_type=f32)


def dot_nt(a, b):
    return lax.dot_general(a, b, (((1,), (1,)), ((), ())), preferred_element_type=f32)


def dot_tn(a, b):
    return lax.dot_general(a, b, (((0,), (0,)), ((), ())), preferred_element_type=f32)


def halves(value):
    high = value.astype(bf16)
    return high, (value - high.astype(f32)).astype(bf16)


def fine_nn(twice, value):
    return dot_nn(twice, jnp.concatenate(halves(value), axis=0))


def fine_tn(a, value):
    both = dot_tn(a, jnp.concatenate(halves(value), axis=1))
    return both[:, : value.shape[1]] + both[:, value.shape[1] :]


def fine_nn_left(value, b):
    high, low = halves(value)
    return dot_nn(high, b) + dot_nn(low, b)


def doubled(hot):
    return jnp.concatenate([hot, hot], axis=1)


def head_sum_matrix(width):
    return jnp.where(
        iota((width, LANES), 0) // HEAD_DIM == iota((width, LANES), 1), 1.0, 0.0
    ).astype(bf16)


def head_spread_matrix(width):
    return jnp.where(
        iota((LANES, width), 1) // HEAD_DIM == iota((LANES, width), 0), 1.0, 0.0
    ).astype(bf16)


def token_hot(x_rows):
    slot = x_rows[:, FEATS : FEATS + 1].astype(f32).astype(i32)
    return jnp.where(iota((x_rows.shape[0], LANES), 1) == slot - 1, 1.0, 0.0).astype(bf16)


def pack_kernel(
    count_ref,
    band_hbm,
    slot_hbm,
    inst_hbm,
    raw_hbm,
    out_hbm,
    band_ref,
    slot_ref,
    inst_ref,
    raw_ref,
    out_ref,
    in_sems,
    out_sems,
):
    moves = [
        pltpu.make_async_copy(src, dst, in_sems.at[k])
        for k, (src, dst) in enumerate(
            (
                (band_hbm, band_ref),
                (raw_hbm, raw_ref),
                (slot_hbm, slot_ref),
                (inst_hbm, inst_ref),
            )
        )
    ]
    for move in moves:
        move.start()
    rows = band_ref.shape[1]
    slots = out_ref.shape[0]
    bands = slots // CAP_ROWS
    earlier = jnp.where(iota((rows, rows), 0) < iota((rows, rows), 1), 1.0, 0.0).astype(bf16)
    moves[0].wait()
    band = band_ref[...]
    live = iota((1, rows), 1) < count_ref[0]
    dest = jnp.where(live, band, -1)
    named = iota((bands, rows), 0) == dest
    hot = jnp.where(named, 1.0, 0.0).astype(bf16)
    before = dot_nn(hot, earlier)
    rank = jnp.sum(jnp.where(named, before, 0.0), axis=0, keepdims=True).astype(i32)
    position = jnp.where(live, band * CAP_ROWS + rank, -1)
    for move in moves[1:]:
        move.wait()
    part = iota((LANES - FEATS, rows), 0)
    meta = jnp.where(
        part == 0,
        (slot_ref[...] + 1).astype(f32),
        jnp.where(part == 1, inst_ref[...].astype(f32), 0.0),
    ).astype(bf16)
    payload = jnp.concatenate([raw_ref[...], meta], axis=0)
    step = slots // out_sems.shape[0]
    leaving = []
    for k in range(out_sems.shape[0]):
        span = pl.ds(k * step, step)
        pick = jnp.where(iota((step, rows), 0) + k * step == position, 1.0, 0.0).astype(bf16)
        out_ref[span, :] = dot_nt(pick, payload).astype(bf16)
        leaving.append(
            pltpu.make_async_copy(out_ref.at[span], out_hbm.at[span], out_sems.at[k])
        )
        leaving[-1].start()
    for move in leaving:
        move.wait()


def ready_kernel(
    tok_ref,
    cot_ref,
    wq_ref,
    zo_ref,
    nk_ref,
    nv_ref,
    gain_ref,
    att_ref,
    query_ref,
    lines_ref,
):
    att_ref[...] = dot_nt(cot_ref[...], zo_ref[...]).astype(bf16)
    query_ref[...] = dot_nn(tok_ref[...], wq_ref[...]).astype(bf16)
    lines_ref[...] = jnp.zeros(lines_ref.shape, f32)
    for row, ref in enumerate((nk_ref, nv_ref, gain_ref)):
        for k in range(ref.shape[0]):
            cols = slice(k * LANES, (k + 1) * LANES)
            lines_ref[row : row + 1, cols] = ref[k : k + 1, :].astype(f32)


def cross_kernel(
    x_ref,
    wk_ref,
    wv_ref,
    table_ref,
    query_ref,
    lines_ref,
    tok_ref,
    cot_ref,
    zq_ref,
    zk_ref,
    zv_ref,
    resid_ref,
    normed_ref,
    key_ref,
    val_ref,
    slope_ref,
    qs_ref,
    tanh_ref,
    prob_ref,
    ntanh_ref,
    nprob_ref,
    lines_out,
    cot_out,
    zq_out,
    zk_out,
    zv_out,
    both_s,
    query_s,
    tok_s,
    keys_s,
    hot_s,
    inst_s,
    weight_s,
    sems,
    key_sem,
):
    slots = x_ref.shape[0]
    feats, width = wk_ref.shape
    kinds = table_ref.shape[0]
    toks = tok_ref.shape[0]
    first = LANES + kinds
    moves = [
        pltpu.make_async_copy(src, dst, sems.at[k])
        for k, (src, dst) in enumerate(
            (
                (wk_ref, both_s.at[:feats, :width]),
                (wv_ref, both_s.at[:feats, width:]),
                (table_ref, both_s.at[LANES:first, width:]),
                (query_ref, query_s),
                (lines_ref, lines_out),
                (tok_ref, tok_s),
                (zq_ref, zq_out),
                (zk_ref, zk_out),
                (zv_ref, zv_out),
                (cot_ref, cot_out),
            )
        )
    ]
    for move in moves[:6]:
        move.start()
    both_s[feats:LANES, :] = jnp.zeros((LANES - feats, 2 * width), bf16)
    both_s[LANES:first, :width] = jnp.zeros((kinds, width), bf16)
    both_s[first:, :] = jnp.zeros((LANES - kinds, 2 * width), bf16)
    head_sum = head_sum_matrix(width)
    head_spread = head_spread_matrix(width)
    for start in range(0, slots, ROW_BLOCK):
        span = pl.ds(start, ROW_BLOCK)
        x = x_ref[span, :]
        hot_s[span, :] = token_hot(x)
        inst = x[:, FEATS + 1 : FEATS + 2].astype(f32).astype(i32)
        inst_s[span, :] = jnp.where(
            iota((ROW_BLOCK, LANES), 1) == inst, 1.0, 0.0
        ).astype(bf16)
    for move in moves[:4]:
        move.wait()
    for move in moves[6:]:
        move.start()
    w_both = both_s[...]
    query = query_s[...]
    total = jnp.zeros((toks, LANES), f32)
    for start in range(0, slots, ROW_BLOCK):
        span = pl.ds(start, ROW_BLOCK)
        hot = hot_s[span, :]
        encoded = dot_nn(jnp.concatenate([x_ref[span, :], inst_s[span, :]], axis=1), w_both)
        keys = encoded[:, :width].astype(bf16)
        keys_s[span, :] = keys
        pre = encoded[:, width:]
        sigma = 0.5 + 0.5 * jnp.tanh(0.5 * pre)
        val_ref[span, :] = (pre * sigma).astype(bf16)
        slope_ref[span, :] = (sigma * (1.0 + pre * (1.0 - sigma))).astype(bf16)
        q_slot = dot_nn(hot, query).astype(bf16)
        qs_ref[span, :] = q_slot
        t = jnp.tanh(dot_nn(q_slot * keys, head_sum) * (score_scale / logit_cap))
        tanh_ref[span, :] = t
        weight = jnp.exp(logit_cap * t)
        weight_s[span, :] = weight
        total = total + fine_tn(hot, weight)
    away = pltpu.make_async_copy(keys_s, key_ref, key_sem)
    away.start()
    for move in moves[4:6]:
        move.wait()
    null_key = lines_out[0:1, :]
    null_val = lines_out[1:2, :]
    gain = lines_out[2:3, :]
    null_t = jnp.tanh(
        fine_nn_left(query.astype(f32) * null_key, head_sum)
        * (score_scale / logit_cap)
    )
    null_weight = jnp.exp(logit_cap * null_t)
    share = 1.0 / (total + null_weight)
    null_prob = null_weight * share
    ntanh_ref[...] = null_t
    nprob_ref[...] = null_prob
    gathered = dot_nn(null_prob.astype(bf16), head_spread) * null_val
    for start in range(0, slots, ROW_BLOCK):
        span = pl.ds(start, ROW_BLOCK)
        hot = hot_s[span, :]
        prob = weight_s[span, :] * fine_nn(doubled(hot), share)
        prob_ref[span, :] = prob
        spread = dot_nn(prob.astype(bf16), head_spread).astype(bf16)
        gathered = gathered + dot_tn(hot, spread * val_ref[span, :])
    resid = (tok_s[...].astype(f32) + gathered).astype(bf16)
    resid_ref[...] = resid
    resid_f = resid.astype(f32)
    inverse = lax.rsqrt(jnp.mean(resid_f * resid_f, axis=1, keepdims=True) + norm_eps)
    normed_ref[...] = (resid_f * inverse * gain).astype(bf16)
    for move in moves[6:]:
        move.wait()
    away.wait()


def zonal_kernel(
    me_ref,
    normed_ref,
    zq_ref,
    zk_ref,
    zv_ref,
    resid_ref,
    cot_ref,
    lines_ref,
    att_ref,
    dres_ref,
    zq_s,
    zk_s,
    zkt_s,
    zv_s,
    att_s,
    norm_s,
    dq_s,
    dk_s,
    dv_s,
    top_s,
    prob_s,
    col_s,
):
    whole, width = normed_ref.shape
    own = resid_ref.shape[0]
    sectors = whole // own
    pairs = width // LANES
    me = me_ref[0]
    for k in range(sectors):
        src = pl.multiple_of(lax.rem(me + k, sectors) * own, own)
        norm_s[k * own : (k + 1) * own, :] = normed_ref[pl.ds(src, own), :]
    normed = norm_s[...]
    for ref, out in ((zq_ref, zq_s), (zk_ref, zk_s), (zv_ref, zv_s)):
        proj = dot_nn(normed, ref[...])
        for p in range(pairs):
            piece = proj[:, p * LANES : (p + 1) * LANES]
            out[p] = piece.astype(bf16)
            if out is zk_s:
                zkt_s[p] = piece.astype(bf16).T
    for k in range(sectors):
        src = pl.multiple_of(lax.rem(me + k, sectors) * own, own)
        part = att_ref[pl.ds(src, own), :]
        for p in range(pairs):
            att_s[p, k * own : (k + 1) * own, :] = part[:, p * LANES : (p + 1) * LANES]
    lane_head = iota((whole, LANES), 1) // HEAD_DIM
    low_half = iota((own, LANES), 1) < HEAD_DIM

    def scores(p):
        keys = zk_s[p]
        vals = zv_s[p]
        for head in range(2):
            rows = slice(head * own, (head + 1) * own)
            qm = jnp.where(lane_head == head, zq_s[p], jnp.zeros((), bf16))
            am = jnp.where(lane_head == head, att_s[p], jnp.zeros((), bf16))
            half = whole // 2
            for start in (0, half):
                cols = slice(start, start + half)
                t = jnp.tanh(dot_nt(keys, qm[cols]) * (score_scale / logit_cap))
                zdp = dot_nt(vals, am[cols])
                weight = jnp.exp2((logit_cap * LOG2E) * t)
                share = 1.0 / jnp.sum(weight, axis=0, keepdims=True)
                inner = jnp.sum(weight * zdp, axis=0, keepdims=True) * share
                t_top = t[:own]
                prob = weight[:own] * share
                top = (prob * (zdp[:own] - inner) * (1.0 - t_top * t_top)).astype(bf16)
                top_s[p, rows, cols] = top
                prob_s[p, rows, cols] = prob.astype(bf16)
                if start == 0:
                    t_rest = t[own:, :own]
                    rest = (
                        (weight[own:, :own] * share[:, :own])
                        * (zdp[own:, :own] - inner[:, :own])
                        * (1.0 - t_rest * t_rest)
                    ).astype(bf16)
                    col_s[p, :own, rows] = top[:, :own]
                    col_s[p, own:, rows] = rest

    def gradients(p):
        dk = dot_nn(top_s[p], zq_s[p])
        dk_s[p] = (jnp.where(low_half, dk[:own], dk[own:]) * score_scale).astype(bf16)
        dv = dot_nn(prob_s[p], att_s[p])
        dv_s[p] = jnp.where(low_half, dv[:own], dv[own:]).astype(bf16)
        dq = dot_nn(zkt_s[p], col_s[p])
        dq_s[p, :HEAD_DIM, :] = dq[:HEAD_DIM, :own] * score_scale
        dq_s[p, HEAD_DIM:, :] = dq[HEAD_DIM:, own:] * score_scale

    for p in range(pairs):
        scores(p)
    for p in range(pairs):
        gradients(p)
    d_zq = jnp.concatenate([dq_s[p].T.astype(bf16) for p in range(pairs)], axis=1)
    d_zk = jnp.concatenate([dk_s[p] for p in range(pairs)], axis=1)
    d_zv = jnp.concatenate([dv_s[p] for p in range(pairs)], axis=1)
    d_normed = (
        dot_nt(d_zq, zq_ref[...]) + dot_nt(d_zk, zk_ref[...]) + dot_nt(d_zv, zv_ref[...])
    )
    resid_f = resid_ref[...].astype(f32)
    inverse = lax.rsqrt(jnp.mean(resid_f * resid_f, axis=1, keepdims=True) + norm_eps)
    gained = lines_ref[2:3, :] * d_normed
    dres_ref[...] = (
        cot_ref[...].astype(f32)
        + inverse * gained
        - resid_f * (inverse * inverse * inverse) * jnp.mean(resid_f * gained, axis=1, keepdims=True)
    ).astype(bf16)


def back_kernel(
    x_ref,
    dres_ref,
    lines_ref,
    val_ref,
    slope_ref,
    qs_ref,
    tanh_ref,
    prob_ref,
    ntanh_ref,
    nprob_ref,
    grad_ref,
    draw_ref,
    nraw_ref,
    ds_s,
    dp_s,
    hot_s,
):
    slots = x_ref.shape[0]
    toks, width = dres_ref.shape
    head_sum = head_sum_matrix(width)
    head_spread = head_spread_matrix(width)
    d_resid = dres_ref[...]
    null_prob = nprob_ref[...]
    null_t = ntanh_ref[...]
    null_dp = fine_nn_left(d_resid.astype(f32) * lines_ref[1:2, :], head_sum)
    inner = null_prob * null_dp
    for start in range(0, slots, ROW_BLOCK):
        span = pl.ds(start, ROW_BLOCK)
        hot = token_hot(x_ref[span, :])
        hot_s[span, :] = hot
        d_slot = dot_nn(hot, d_resid).astype(bf16)
        ds_s[span, :] = d_slot
        dp = dot_nn(d_slot * val_ref[span, :], head_sum)
        dp_s[span, :] = dp
        inner = inner + fine_tn(hot, prob_ref[span, :] * dp)
    nraw_ref[...] = null_prob * (null_dp - inner) * (1.0 - null_t * null_t) * score_scale
    grads = jnp.zeros((LANES, 2 * width), f32)
    for start in range(0, slots, ROW_BLOCK):
        span = pl.ds(start, ROW_BLOCK)
        prob = prob_ref[span, :]
        t = tanh_ref[span, :]
        d_raw = (
            prob
            * (dp_s[span, :] - fine_nn(doubled(hot_s[span, :]), inner))
            * (1.0 - t * t)
            * score_scale
        ).astype(bf16)
        draw_ref[span, :] = d_raw
        d_raw_wide = dot_nn(d_raw, head_spread).astype(bf16)
        prob_wide = dot_nn(prob.astype(bf16), head_spread).astype(bf16)
        d_keys = d_raw_wide * qs_ref[span, :]
        d_pre = (prob_wide * ds_s[span, :]) * slope_ref[span, :]
        grads = grads + dot_tn(x_ref[span, :], jnp.concatenate([d_keys, d_pre], axis=1))
    blocks = 2 * width // LANES
    for b in range(blocks):
        grad_ref[b * FEATS : (b + 1) * FEATS, :] = grads[
            :FEATS, b * LANES : (b + 1) * LANES
        ].astype(bf16)
    spare = grad_ref.shape[0] - blocks * FEATS
    grad_ref[blocks * FEATS :, :] = jnp.zeros((spare, LANES), bf16)


def token_kernel(
    x_ref,
    dres_ref,
    lines_ref,
    draw_ref,
    nraw_ref,
    key_ref,
    wq_ref,
    dtok_ref,
    keys_s,
    wq_s,
    sems,
):
    slots = x_ref.shape[0]
    keys_move = pltpu.make_async_copy(key_ref, keys_s, sems.at[0])
    wq_move = pltpu.make_async_copy(wq_ref, wq_s, sems.at[1])
    keys_move.start()
    wq_move.start()
    head_spread = head_spread_matrix(dres_ref.shape[1])
    d_query = fine_nn_left(nraw_ref[...], head_spread) * lines_ref[0:1, :]
    keys_move.wait()
    for start in range(0, slots, ROW_BLOCK):
        span = pl.ds(start, ROW_BLOCK)
        d_raw_wide = dot_nn(draw_ref[span, :], head_spread).astype(bf16)
        hot = token_hot(x_ref[span, :])
        d_query = d_query + dot_tn(hot, d_raw_wide * keys_s[span, :])
    wq_move.wait()
    d_tok = dres_ref[...].astype(f32) + dot_nt(d_query.astype(bf16), wq_s[...])
    dtok_ref[...] = d_tok.astype(bf16)


def in_vmem(value):
    return pltpu.with_memory_space_constraint(value, pltpu.VMEM)


def unpack_kernel(scale, parts_ref, key_ref, value_ref):
    width = key_ref.shape[1]
    pieces = width // LANES
    for g, out in enumerate((key_ref, value_ref)):
        for b in range(pieces):
            start = (g * pieces + b) * FEATS
            rows = parts_ref[start : start + FEATS, :].astype(f32)
            out[:, b * LANES : (b + 1) * LANES] = rows * scale


def in_hbm(value):
    return pltpu.with_memory_space_constraint(value, pltpu.HBM)


def whole_call(
    kernel, name, out_shape, args, scalars=0, fetched=0, far=0, away=(), scratch=(), scoped=16
):
    smem = pl.BlockSpec(memory_space=pltpu.SMEM)
    vmem = pl.BlockSpec(memory_space=pltpu.VMEM)
    hbm = pl.BlockSpec(memory_space=pltpu.HBM)
    several = isinstance(out_shape, (list, tuple))
    first, last = scalars + fetched, len(args) - far
    args = (
        tuple(args[:scalars])
        + tuple(in_hbm(a) for a in args[scalars:first])
        + tuple(in_vmem(a) for a in args[first:last])
        + tuple(in_hbm(a) for a in args[last:])
    )
    return pl.pallas_call(
        kernel,
        name=name,
        out_shape=out_shape,
        in_specs=[smem] * scalars + [vmem] * (last - scalars) + [hbm] * far,
        out_specs=[hbm if k in away else vmem for k in range(len(out_shape))]
        if several
        else vmem,
        scratch_shapes=list(scratch),
        compiler_params=pltpu.CompilerParams(vmem_limit_bytes=scoped * 1024 * 1024),
    )(*args)


def plain(rows, cols, dtype):
    return jax.ShapeDtypeStruct((rows, cols), dtype)


def shaped(rows, cols, dtype):
    return pltpu.VMEM((rows, cols), dtype)


def pack(obs_count, obs_band, obs_slot, obs_inst, raw_obs, bands):
    rows, feats = raw_obs.shape
    slots = bands * CAP_ROWS
    line = pltpu.VMEM((1, rows), i32)
    return whole_call(
        pack_kernel,
        "pack",
        [plain(slots, LANES, bf16)],
        (
            obs_count,
            obs_band.reshape(1, rows),
            obs_slot.reshape(1, rows),
            obs_inst.reshape(1, rows),
            raw_obs.T,
        ),
        scalars=1,
        far=4,
        away=(0,),
        scratch=(
            line,
            line,
            line,
            pltpu.VMEM((feats, rows), bf16),
            pltpu.VMEM((slots, LANES), bf16),
            pltpu.SemaphoreType.DMA((4,)),
            pltpu.SemaphoreType.DMA((4,)),
        ),
    )[0]


def get_ready(tok, cot, w_query, zonal_out, null_key, null_val, gain):
    toks, width = tok.shape
    args = (tok, cot, w_query, zonal_out) + tuple(
        v.reshape(width // LANES, LANES) for v in (null_key, null_val, gain)
    )
    return whole_call(
        ready_kernel,
        "get_ready",
        [
            plain(toks, width, bf16),
            pltpu.HBM((toks, width), bf16),
            pltpu.HBM((8, width), f32),
        ],
        args,
        fetched=len(args),
    )


def cross_forward(x, w_key, w_val, table, query, lines, tok, cot, zq, zk, zv):
    slots = x.shape[0]
    toks, width = tok.shape
    big = shaped(slots, width, bf16)
    small = shaped(slots, LANES, f32)
    null = shaped(toks, LANES, f32)
    row = shaped(toks, width, bf16)
    square = shaped(*zq.shape, bf16)
    far = (w_key, w_val, table, query, lines, tok, cot, zq, zk, zv)
    return whole_call(
        cross_kernel,
        "cross_forward",
        [row, row, pltpu.HBM((slots, width), bf16), big, big, big, small, small, null, null]
        + [shaped(*lines.shape, f32), row, square, square, square],
        (x,) + far,
        far=len(far),
        away=(2,),
        scratch=(
            pltpu.VMEM((2 * LANES, 2 * width), bf16),
            pltpu.VMEM((toks, width), bf16),
            pltpu.VMEM((toks, width), bf16),
            pltpu.VMEM((slots, width), bf16),
            pltpu.VMEM((slots, LANES), bf16),
            pltpu.VMEM((slots, LANES), bf16),
            pltpu.VMEM((slots, LANES), f32),
            pltpu.SemaphoreType.DMA((len(far),)),
            pltpu.SemaphoreType.DMA(()),
        ),
    )


def zonal(me, normed_all, att_all, zq, zk, zv, resid, cot, lines):
    own, width = resid.shape
    whole = normed_all.shape[0]
    pairs = width // LANES
    rows = pltpu.VMEM((pairs, whole, LANES), bf16)
    return whole_call(
        zonal_kernel,
        "zonal",
        shaped(own, width, bf16),
        (me, normed_all, zq, zk, zv, resid, cot, lines, att_all),
        scalars=1,
        scratch=(
            rows,
            rows,
            pltpu.VMEM((pairs, LANES, whole), bf16),
            rows,
            rows,
            pltpu.VMEM((whole, width), bf16),
            pltpu.VMEM((pairs, LANES, own), f32),
            pltpu.VMEM((pairs, own, LANES), bf16),
            pltpu.VMEM((pairs, own, LANES), bf16),
            pltpu.VMEM((pairs, 2 * own, whole), bf16),
            pltpu.VMEM((pairs, 2 * own, whole), bf16),
            pltpu.VMEM((pairs, whole, 2 * own), bf16),
        ),
    )


def cross_backward(x, d_resid, lines, saved):
    slots = x.shape[0]
    toks, width = d_resid.shape
    return whole_call(
        back_kernel,
        "cross_backward",
        [
            shaped(PLANE * CHUNK, LANES, bf16),
            shaped(slots, LANES, bf16),
            shaped(toks, LANES, f32),
        ],
        (x, d_resid, lines) + tuple(saved),
        scratch=(
            pltpu.VMEM((slots, width), bf16),
            pltpu.VMEM((slots, LANES), f32),
            pltpu.VMEM((slots, LANES), bf16),
        ),
    )


def token_gradient(x, d_resid, lines, keys, d_raw, null_raw, w_query):
    return whole_call(
        token_kernel,
        "token_gradient",
        plain(*d_resid.shape, bf16),
        (x, d_resid, lines, d_raw, null_raw, keys, w_query),
        far=2,
        scratch=(
            pltpu.VMEM(keys.shape, bf16),
            pltpu.VMEM(w_query.shape, bf16),
            pltpu.SemaphoreType.DMA((2,)),
        ),
    )


def unpack(parts, width, scale):
    out = plain(FEATS, width, f32)
    return whole_call(
        functools.partial(unpack_kernel, scale), "unpack", [out, out], (parts,)
    )


def sum_everywhere(rows):
    plane = [list(range(z * PLANE, (z + 1) * PLANE)) for z in range(DEPTH)]
    lats = PLANE // 4
    column = [[z * lats + k for z in range(DEPTH)] for k in range(lats)]

    def swap(parts, axes, groups):
        return lax.all_to_all(
            parts, axes, split_axis=0, concat_axis=0, tiled=True, axis_index_groups=groups
        )

    def total(parts):
        return jnp.sum(parts.astype(f32), axis=0)

    parts = swap(rows.reshape(PLANE, CHUNK, LANES), ("lat", "lon"), plane)
    mine = total(parts).astype(bf16)
    parts = swap(jnp.broadcast_to(mine, (DEPTH, CHUNK, LANES)), "lat", column)
    mine = total(parts).astype(bf16)
    parts = swap(jnp.broadcast_to(mine, (PLANE, CHUNK, LANES)), ("lat", "lon"), plane)
    return parts.reshape(PLANE * CHUNK, LANES)


def on_device(
    tokens,
    cotangent,
    raw_obs,
    obs_band,
    obs_slot,
    obs_inst,
    obs_count,
    w_key_obs,
    w_val_obs,
    inst_table,
    null_key,
    null_val,
    w_query,
    norm_gain,
    zonal_query,
    zonal_key,
    zonal_value,
    zonal_out,
):
    tok_rows, width = tokens.shape[1:]
    bands = lax.axis_size("lat")
    devices = bands * lax.axis_size("lon")
    obs_total = raw_obs.shape[0] * devices
    tok = tokens.reshape(tok_rows, width)
    cot = cotangent.reshape(tok_rows, width)
    packed = pack(obs_count, obs_band, obs_slot, obs_inst, raw_obs, bands)
    received = lax.all_to_all(
        packed.reshape(bands, CAP_ROWS, LANES), "lat", split_axis=0, concat_axis=0, tiled=True
    ).reshape(bands * CAP_ROWS, LANES)
    d_att, query, lines = get_ready(
        tok, cot, w_query, zonal_out, null_key, null_val, norm_gain
    )
    att_all = lax.all_gather(d_att, "lon", axis=0, tiled=True)
    resid, normed, keys, *saved, lines, cot, zq, zk, zv = cross_forward(
        received,
        w_key_obs,
        w_val_obs,
        inst_table,
        query,
        lines,
        tok,
        cot,
        zonal_query,
        zonal_key,
        zonal_value,
    )
    normed_all = lax.all_gather(normed, "lon", axis=0, tiled=True)
    me = lax.axis_index("lon").astype(i32).reshape(1)
    d_resid = zonal(me, normed_all, att_all, zq, zk, zv, resid, cot, lines)
    grads, d_raw, null_raw = cross_backward(received, d_resid, lines, saved)
    d_tok = token_gradient(received, d_resid, lines, keys, d_raw, null_raw, w_query)
    key_grad, value_grad = unpack(sum_everywhere(grads), width, 1.0 / math.sqrt(obs_total))
    return d_tok.reshape(1, tok_rows, width), key_grad, value_grad


def solution(mesh):
    return jax.shard_map(
        on_device,
        mesh=mesh,
        in_specs=(
            P("lat", "lon", None),
            P("lat", "lon", None),
            P(("lat", "lon"), None),
            P(("lat", "lon"), None),
            P(("lat", "lon")),
            P(("lat", "lon")),
            P(("lat", "lon")),
            P(),
            P(),
            P(),
            P(),
            P(),
            P(),
            P(),
            P(),
            P(),
            P(),
            P(),
        ),
        out_specs=(P("lat", "lon", None), P(), P()),
        check_vma=False,
    )
```

```python
import functools
import math

import jax
import jax.numpy as jnp
from jax import lax
from jax.experimental import pallas as pl
from jax.experimental.pallas import tpu as pltpu
from jax.sharding import PartitionSpec as P

HEAD_DIM = 64
CAP_ROWS = 8
LANES = 128
FEATS = 64

logit_cap = 6.0
norm_eps = 1e-06
score_scale = 1.0 / math.sqrt(HEAD_DIM)
LOG2E = math.log2(math.e)

bf16 = jnp.bfloat16
f32 = jnp.float32
i32 = jnp.int32

PLANE = 32
DEPTH = 16
CHUNK = 24
ROW_BLOCK = 1024


def iota(shape, dim):
    return lax.broadcasted_iota(i32, shape, dim)


def dot_nn(a, b):
    return lax.dot_general(a, b, (((1,), (0,)), ((), ())), preferred_element_type=f32)


def dot_nt(a, b):
    return lax.dot_general(a, b, (((1,), (1,)), ((), ())), preferred_element_type=f32)


def dot_tn(a, b):
    return lax.dot_general(a, b, (((0,), (0,)), ((), ())), preferred_element_type=f32)


def halves(value):
    high = value.astype(bf16)
    return high, (value - high.astype(f32)).astype(bf16)


def fine_nn(twice, value):
    return dot_nn(twice, jnp.concatenate(halves(value), axis=0))


def fine_tn(a, value):
    both = dot_tn(a, jnp.concatenate(halves(value), axis=1))
    return both[:, : value.shape[1]] + both[:, value.shape[1] :]


def fine_nn_left(value, b):
    high, low = halves(value)
    return dot_nn(high, b) + dot_nn(low, b)


def doubled(hot):
    return jnp.concatenate([hot, hot], axis=1)


def head_sum_matrix(width):
    return jnp.where(
        iota((width, LANES), 0) // HEAD_DIM == iota((width, LANES), 1), 1.0, 0.0
    ).astype(bf16)


def head_spread_matrix(width):
    return jnp.where(
        iota((LANES, width), 1) // HEAD_DIM == iota((LANES, width), 0), 1.0, 0.0
    ).astype(bf16)


def token_hot(x_rows):
    slot = x_rows[:, FEATS : FEATS + 1].astype(f32).astype(i32)
    return jnp.where(iota((x_rows.shape[0], LANES), 1) == slot - 1, 1.0, 0.0).astype(bf16)


def pack_kernel(
    count_ref,
    band_hbm,
    slot_hbm,
    inst_hbm,
    raw_hbm,
    out_hbm,
    band_ref,
    slot_ref,
    inst_ref,
    raw_ref,
    out_ref,
    in_sems,
    out_sems,
):
    moves = [
        pltpu.make_async_copy(src, dst, in_sems.at[k])
        for k, (src, dst) in enumerate(
            (
                (band_hbm, band_ref),
                (raw_hbm, raw_ref),
                (slot_hbm, slot_ref),
                (inst_hbm, inst_ref),
            )
        )
    ]
    for move in moves:
        move.start()
    rows = band_ref.shape[1]
    slots = out_ref.shape[0]
    bands = slots // CAP_ROWS
    earlier = jnp.where(iota((rows, rows), 0) < iota((rows, rows), 1), 1.0, 0.0).astype(bf16)
    moves[0].wait()
    band = band_ref[...]
    live = iota((1, rows), 1) < count_ref[0]
    dest = jnp.where(live, band, -1)
    named = iota((bands, rows), 0) == dest
    hot = jnp.where(named, 1.0, 0.0).astype(bf16)
    before = dot_nn(hot, earlier)
    rank = jnp.sum(jnp.where(named, before, 0.0), axis=0, keepdims=True).astype(i32)
    position = jnp.where(live, band * CAP_ROWS + rank, -1)
    for move in moves[1:]:
        move.wait()
    part = iota((LANES - FEATS, rows), 0)
    meta = jnp.where(
        part == 0,
        (slot_ref[...] + 1).astype(f32),
        jnp.where(part == 1, inst_ref[...].astype(f32), 0.0),
    ).astype(bf16)
    payload = jnp.concatenate([raw_ref[...], meta], axis=0)
    step = slots // out_sems.shape[0]
    leaving = []
    for k in range(out_sems.shape[0]):
        span = pl.ds(k * step, step)
        pick = jnp.where(iota((step, rows), 0) + k * step == position, 1.0, 0.0).astype(bf16)
        out_ref[span, :] = dot_nt(pick, payload).astype(bf16)
        leaving.append(
            pltpu.make_async_copy(out_ref.at[span], out_hbm.at[span], out_sems.at[k])
        )
        leaving[-1].start()
    for move in leaving:
        move.wait()


def ready_kernel(
    tok_ref,
    cot_ref,
    wq_ref,
    zo_ref,
    nk_ref,
    nv_ref,
    gain_ref,
    att_ref,
    query_ref,
    lines_ref,
):
    att_ref[...] = dot_nt(cot_ref[...], zo_ref[...]).astype(bf16).astype(f32)
    query_ref[...] = dot_nn(tok_ref[...], wq_ref[...]).astype(bf16)
    lines_ref[...] = jnp.zeros(lines_ref.shape, f32)
    for row, ref in enumerate((nk_ref, nv_ref, gain_ref)):
        for k in range(ref.shape[0]):
            cols = slice(k * LANES, (k + 1) * LANES)
            lines_ref[row : row + 1, cols] = ref[k : k + 1, :].astype(f32)


def cross_kernel(
    x_ref,
    wk_ref,
    wv_ref,
    table_ref,
    query_ref,
    lines_ref,
    tok_ref,
    cot_ref,
    zq_ref,
    zk_ref,
    zv_ref,
    att_ref,
    resid_ref,
    normed_ref,
    key_ref,
    val_ref,
    slope_ref,
    qs_ref,
    tanh_ref,
    prob_ref,
    ntanh_ref,
    nprob_ref,
    lines_out,
    cot_out,
    zq_out,
    zk_out,
    zv_out,
    att_out,
    both_s,
    query_s,
    tok_s,
    keys_s,
    hot_s,
    inst_s,
    weight_s,
    sems,
    key_sem,
):
    slots = x_ref.shape[0]
    feats, width = wk_ref.shape
    kinds = table_ref.shape[0]
    toks = tok_ref.shape[0]
    first = LANES + kinds
    moves = [
        pltpu.make_async_copy(src, dst, sems.at[k])
        for k, (src, dst) in enumerate(
            (
                (wk_ref, both_s.at[:feats, :width]),
                (wv_ref, both_s.at[:feats, width:]),
                (table_ref, both_s.at[LANES:first, width:]),
                (query_ref, query_s),
                (lines_ref, lines_out),
                (tok_ref, tok_s),
                (zq_ref, zq_out),
                (zk_ref, zk_out),
                (zv_ref, zv_out),
                (cot_ref, cot_out),
                (att_ref, att_out),
            )
        )
    ]
    for move in moves[:6]:
        move.start()
    both_s[feats:LANES, :] = jnp.zeros((LANES - feats, 2 * width), bf16)
    both_s[LANES:first, :width] = jnp.zeros((kinds, width), bf16)
    both_s[first:, :] = jnp.zeros((LANES - kinds, 2 * width), bf16)
    head_sum = head_sum_matrix(width)
    head_spread = head_spread_matrix(width)
    for start in range(0, slots, ROW_BLOCK):
        span = pl.ds(start, ROW_BLOCK)
        x = x_ref[span, :]
        hot_s[span, :] = token_hot(x)
        inst = x[:, FEATS + 1 : FEATS + 2].astype(f32).astype(i32)
        inst_s[span, :] = jnp.where(
            iota((ROW_BLOCK, LANES), 1) == inst, 1.0, 0.0
        ).astype(bf16)
    for move in moves[:4]:
        move.wait()
    for move in moves[6:]:
        move.start()
    w_both = both_s[...]
    query = query_s[...]
    total = jnp.zeros((toks, LANES), f32)
    for start in range(0, slots, ROW_BLOCK):
        span = pl.ds(start, ROW_BLOCK)
        hot = hot_s[span, :]
        encoded = dot_nn(jnp.concatenate([x_ref[span, :], inst_s[span, :]], axis=1), w_both)
        keys = encoded[:, :width].astype(bf16)
        keys_s[span, :] = keys
        pre = encoded[:, width:]
        sigma = 0.5 + 0.5 * jnp.tanh(0.5 * pre)
        val_ref[span, :] = (pre * sigma).astype(bf16)
        slope_ref[span, :] = (sigma * (1.0 + pre * (1.0 - sigma))).astype(bf16)
        q_slot = dot_nn(hot, query).astype(bf16)
        qs_ref[span, :] = q_slot
        t = jnp.tanh(dot_nn(q_slot * keys, head_sum) * (score_scale / logit_cap))
        tanh_ref[span, :] = t
        weight = jnp.exp(logit_cap * t)
        weight_s[span, :] = weight
        total = total + fine_tn(hot, weight)
    away = pltpu.make_async_copy(keys_s, key_ref, key_sem)
    away.start()
    for move in moves[4:6]:
        move.wait()
    null_key = lines_out[0:1, :]
    null_val = lines_out[1:2, :]
    gain = lines_out[2:3, :]
    null_t = jnp.tanh(
        fine_nn_left(query.astype(f32) * null_key, head_sum)
        * (score_scale / logit_cap)
    )
    null_weight = jnp.exp(logit_cap * null_t)
    share = 1.0 / (total + null_weight)
    null_prob = null_weight * share
    ntanh_ref[...] = null_t
    nprob_ref[...] = null_prob
    gathered = dot_nn(null_prob.astype(bf16), head_spread) * null_val
    for start in range(0, slots, ROW_BLOCK):
        span = pl.ds(start, ROW_BLOCK)
        hot = hot_s[span, :]
        prob = weight_s[span, :] * fine_nn(doubled(hot), share)
        prob_ref[span, :] = prob
        spread = dot_nn(prob.astype(bf16), head_spread).astype(bf16)
        gathered = gathered + dot_tn(hot, spread * val_ref[span, :])
    resid = (tok_s[...].astype(f32) + gathered).astype(bf16)
    resid_ref[...] = resid
    resid_f = resid.astype(f32)
    inverse = lax.rsqrt(jnp.mean(resid_f * resid_f, axis=1, keepdims=True) + norm_eps)
    normed_ref[...] = (resid_f * inverse * gain).astype(bf16)
    for move in moves[6:]:
        move.wait()
    away.wait()


def zonal_kernel(
    me_ref,
    normed_ref,
    zq_ref,
    zk_ref,
    zv_ref,
    resid_ref,
    cot_ref,
    lines_ref,
    att_ref,
    dres_ref,
    zq_s,
    zk_s,
    zkt_s,
    zv_s,
    att_s,
    norm_s,
    dq_s,
    dk_s,
    dv_s,
    top_s,
    prob_s,
    col_s,
):
    whole, width = normed_ref.shape
    own = resid_ref.shape[0]
    sectors = whole // own
    pairs = width // LANES
    me = me_ref[0]
    for k in range(sectors):
        src = pl.multiple_of(lax.rem(me + k, sectors) * own, own)
        norm_s[k * own : (k + 1) * own, :] = normed_ref[pl.ds(src, own), :]
    normed = norm_s[...]
    for ref, out in ((zq_ref, zq_s), (zk_ref, zk_s), (zv_ref, zv_s)):
        proj = dot_nn(normed, ref[...])
        for p in range(pairs):
            piece = proj[:, p * LANES : (p + 1) * LANES]
            out[p] = piece.astype(bf16)
            if out is zk_s:
                zkt_s[p] = piece.astype(bf16).T
    for k in range(sectors):
        src = pl.multiple_of(lax.rem(me + k, sectors) * own, own)
        part = att_ref[pl.ds(src, own), :].astype(bf16)
        for p in range(pairs):
            att_s[p, k * own : (k + 1) * own, :] = part[:, p * LANES : (p + 1) * LANES]
    lane_head = iota((whole, LANES), 1) // HEAD_DIM
    low_half = iota((own, LANES), 1) < HEAD_DIM

    def scores(p):
        keys = zk_s[p]
        vals = zv_s[p]
        for head in range(2):
            rows = slice(head * own, (head + 1) * own)
            qm = jnp.where(lane_head == head, zq_s[p], jnp.zeros((), bf16))
            am = jnp.where(lane_head == head, att_s[p], jnp.zeros((), bf16))
            half = whole // 2
            for start in (0, half):
                cols = slice(start, start + half)
                t = jnp.tanh(dot_nt(keys, qm[cols]) * (score_scale / logit_cap))
                zdp = dot_nt(vals, am[cols])
                weight = jnp.exp2((logit_cap * LOG2E) * t)
                share = 1.0 / jnp.sum(weight, axis=0, keepdims=True)
                inner = jnp.sum(weight * zdp, axis=0, keepdims=True) * share
                t_top = t[:own]
                prob = weight[:own] * share
                top = (prob * (zdp[:own] - inner) * (1.0 - t_top * t_top)).astype(bf16)
                top_s[p, rows, cols] = top
                prob_s[p, rows, cols] = prob.astype(bf16)
                if start == 0:
                    t_rest = t[own:, :own]
                    rest = (
                        (weight[own:, :own] * share[:, :own])
                        * (zdp[own:, :own] - inner[:, :own])
                        * (1.0 - t_rest * t_rest)
                    ).astype(bf16)
                    col_s[p, :own, rows] = top[:, :own]
                    col_s[p, own:, rows] = rest

    def gradients(p):
        dk = dot_nn(top_s[p], zq_s[p])
        dk_s[p] = (jnp.where(low_half, dk[:own], dk[own:]) * score_scale).astype(bf16)
        dv = dot_nn(prob_s[p], att_s[p])
        dv_s[p] = jnp.where(low_half, dv[:own], dv[own:]).astype(bf16)
        dq = dot_nn(zkt_s[p], col_s[p])
        dq_s[p, :HEAD_DIM, :] = dq[:HEAD_DIM, :own] * score_scale
        dq_s[p, HEAD_DIM:, :] = dq[HEAD_DIM:, own:] * score_scale

    for p in range(pairs):
        scores(p)
    for p in range(pairs):
        gradients(p)
    d_zq = jnp.concatenate([dq_s[p].T.astype(bf16) for p in range(pairs)], axis=1)
    d_zk = jnp.concatenate([dk_s[p] for p in range(pairs)], axis=1)
    d_zv = jnp.concatenate([dv_s[p] for p in range(pairs)], axis=1)
    d_normed = (
        dot_nt(d_zq, zq_ref[...]) + dot_nt(d_zk, zk_ref[...]) + dot_nt(d_zv, zv_ref[...])
    )
    resid_f = resid_ref[...].astype(f32)
    inverse = lax.rsqrt(jnp.mean(resid_f * resid_f, axis=1, keepdims=True) + norm_eps)
    gained = lines_ref[2:3, :] * d_normed
    dres_ref[...] = (
        cot_ref[...].astype(f32)
        + inverse * gained
        - resid_f * (inverse * inverse * inverse) * jnp.mean(resid_f * gained, axis=1, keepdims=True)
    ).astype(bf16)


def back_kernel(
    x_ref,
    dres_ref,
    lines_ref,
    val_ref,
    slope_ref,
    qs_ref,
    tanh_ref,
    prob_ref,
    ntanh_ref,
    nprob_ref,
    grad_ref,
    draw_ref,
    nraw_ref,
    ds_s,
    dp_s,
    hot_s,
):
    slots = x_ref.shape[0]
    toks, width = dres_ref.shape
    head_sum = head_sum_matrix(width)
    head_spread = head_spread_matrix(width)
    d_resid = dres_ref[...]
    null_prob = nprob_ref[...]
    null_t = ntanh_ref[...]
    null_dp = fine_nn_left(d_resid.astype(f32) * lines_ref[1:2, :], head_sum)
    inner = null_prob * null_dp
    for start in range(0, slots, ROW_BLOCK):
        span = pl.ds(start, ROW_BLOCK)
        hot = token_hot(x_ref[span, :])
        hot_s[span, :] = hot
        d_slot = dot_nn(hot, d_resid).astype(bf16)
        ds_s[span, :] = d_slot
        dp = dot_nn(d_slot * val_ref[span, :], head_sum)
        dp_s[span, :] = dp
        inner = inner + fine_tn(hot, prob_ref[span, :] * dp)
    nraw_ref[...] = null_prob * (null_dp - inner) * (1.0 - null_t * null_t) * score_scale
    grads = jnp.zeros((LANES, 2 * width), f32)
    for start in range(0, slots, ROW_BLOCK):
        span = pl.ds(start, ROW_BLOCK)
        prob = prob_ref[span, :]
        t = tanh_ref[span, :]
        d_raw = (
            prob
            * (dp_s[span, :] - fine_nn(doubled(hot_s[span, :]), inner))
            * (1.0 - t * t)
            * score_scale
        ).astype(bf16)
        draw_ref[span, :] = d_raw
        d_raw_wide = dot_nn(d_raw, head_spread).astype(bf16)
        prob_wide = dot_nn(prob.astype(bf16), head_spread).astype(bf16)
        d_keys = d_raw_wide * qs_ref[span, :]
        d_pre = (prob_wide * ds_s[span, :]) * slope_ref[span, :]
        grads = grads + dot_tn(x_ref[span, :], jnp.concatenate([d_keys, d_pre], axis=1))
    blocks = 2 * width // LANES
    for b in range(blocks):
        grad_ref[b * FEATS : (b + 1) * FEATS, :] = grads[
            :FEATS, b * LANES : (b + 1) * LANES
        ].astype(bf16)
    spare = grad_ref.shape[0] - blocks * FEATS
    grad_ref[blocks * FEATS :, :] = jnp.zeros((spare, LANES), bf16)


def token_kernel(
    x_ref,
    dres_ref,
    lines_ref,
    draw_ref,
    nraw_ref,
    key_ref,
    wq_ref,
    dtok_ref,
    keys_s,
    wq_s,
    sems,
):
    slots = x_ref.shape[0]
    keys_move = pltpu.make_async_copy(key_ref, keys_s, sems.at[0])
    wq_move = pltpu.make_async_copy(wq_ref, wq_s, sems.at[1])
    keys_move.start()
    wq_move.start()
    head_spread = head_spread_matrix(dres_ref.shape[1])
    d_query = fine_nn_left(nraw_ref[...], head_spread) * lines_ref[0:1, :]
    keys_move.wait()
    for start in range(0, slots, ROW_BLOCK):
        span = pl.ds(start, ROW_BLOCK)
        d_raw_wide = dot_nn(draw_ref[span, :], head_spread).astype(bf16)
        hot = token_hot(x_ref[span, :])
        d_query = d_query + dot_tn(hot, d_raw_wide * keys_s[span, :])
    wq_move.wait()
    d_tok = dres_ref[...].astype(f32) + dot_nt(d_query.astype(bf16), wq_s[...])
    dtok_ref[...] = d_tok.astype(bf16)


def in_vmem(value):
    return pltpu.with_memory_space_constraint(value, pltpu.VMEM)


def unpack_kernel(scale, parts_ref, key_ref, value_ref):
    width = key_ref.shape[1]
    pieces = width // LANES
    for g, out in enumerate((key_ref, value_ref)):
        for b in range(pieces):
            start = (g * pieces + b) * FEATS
            rows = parts_ref[start : start + FEATS, :].astype(f32)
            out[:, b * LANES : (b + 1) * LANES] = rows * scale


def in_hbm(value):
    return pltpu.with_memory_space_constraint(value, pltpu.HBM)


def whole_call(
    kernel, name, out_shape, args, scalars=0, fetched=0, far=0, away=(), scratch=(), scoped=16
):
    smem = pl.BlockSpec(memory_space=pltpu.SMEM)
    vmem = pl.BlockSpec(memory_space=pltpu.VMEM)
    hbm = pl.BlockSpec(memory_space=pltpu.HBM)
    several = isinstance(out_shape, (list, tuple))
    first, last = scalars + fetched, len(args) - far
    args = (
        tuple(args[:scalars])
        + tuple(in_hbm(a) for a in args[scalars:first])
        + tuple(in_vmem(a) for a in args[first:last])
        + tuple(in_hbm(a) for a in args[last:])
    )
    return pl.pallas_call(
        kernel,
        name=name,
        out_shape=out_shape,
        in_specs=[smem] * scalars + [vmem] * (last - scalars) + [hbm] * far,
        out_specs=[hbm if k in away else vmem for k in range(len(out_shape))]
        if several
        else vmem,
        scratch_shapes=list(scratch),
        compiler_params=pltpu.CompilerParams(vmem_limit_bytes=scoped * 1024 * 1024),
    )(*args)


def plain(rows, cols, dtype):
    return jax.ShapeDtypeStruct((rows, cols), dtype)


def shaped(rows, cols, dtype):
    return pltpu.VMEM((rows, cols), dtype)


def pack(obs_count, obs_band, obs_slot, obs_inst, raw_obs, bands):
    rows, feats = raw_obs.shape
    slots = bands * CAP_ROWS
    line = pltpu.VMEM((1, rows), i32)
    return whole_call(
        pack_kernel,
        "pack",
        [plain(slots, LANES, bf16)],
        (
            obs_count,
            obs_band.reshape(1, rows),
            obs_slot.reshape(1, rows),
            obs_inst.reshape(1, rows),
            raw_obs.T,
        ),
        scalars=1,
        far=4,
        away=(0,),
        scratch=(
            line,
            line,
            line,
            pltpu.VMEM((feats, rows), bf16),
            pltpu.VMEM((slots, LANES), bf16),
            pltpu.SemaphoreType.DMA((4,)),
            pltpu.SemaphoreType.DMA((4,)),
        ),
    )[0]


def get_ready(tok, cot, w_query, zonal_out, null_key, null_val, gain):
    toks, width = tok.shape
    args = (tok, cot, w_query, zonal_out) + tuple(
        v.reshape(width // LANES, LANES) for v in (null_key, null_val, gain)
    )
    return whole_call(
        ready_kernel,
        "get_ready",
        [
            pltpu.HBM((toks, width), f32),
            pltpu.HBM((toks, width), bf16),
            pltpu.HBM((8, width), f32),
        ],
        args,
        fetched=len(args),
    )


def cross_forward(x, w_key, w_val, table, query, lines, tok, cot, zq, zk, zv, att):
    slots = x.shape[0]
    toks, width = tok.shape
    big = shaped(slots, width, bf16)
    small = shaped(slots, LANES, f32)
    null = shaped(toks, LANES, f32)
    row = shaped(toks, width, bf16)
    square = shaped(*zq.shape, bf16)
    far = (w_key, w_val, table, query, lines, tok, cot, zq, zk, zv, att)
    return whole_call(
        cross_kernel,
        "cross_forward",
        [row, row, pltpu.HBM((slots, width), bf16), big, big, big, small, small, null, null]
        + [shaped(*lines.shape, f32), row, square, square, square]
        + [shaped(*att.shape, f32)],
        (x,) + far,
        far=len(far),
        away=(2,),
        scratch=(
            pltpu.VMEM((2 * LANES, 2 * width), bf16),
            pltpu.VMEM((toks, width), bf16),
            pltpu.VMEM((toks, width), bf16),
            pltpu.VMEM((slots, width), bf16),
            pltpu.VMEM((slots, LANES), bf16),
            pltpu.VMEM((slots, LANES), bf16),
            pltpu.VMEM((slots, LANES), f32),
            pltpu.SemaphoreType.DMA((len(far),)),
            pltpu.SemaphoreType.DMA(()),
        ),
    )


def zonal(me, normed_all, att_all, zq, zk, zv, resid, cot, lines):
    own, width = resid.shape
    whole = normed_all.shape[0]
    pairs = width // LANES
    rows = pltpu.VMEM((pairs, whole, LANES), bf16)
    return whole_call(
        zonal_kernel,
        "zonal",
        shaped(own, width, bf16),
        (me, normed_all, zq, zk, zv, resid, cot, lines, att_all),
        scalars=1,
        scratch=(
            rows,
            rows,
            pltpu.VMEM((pairs, LANES, whole), bf16),
            rows,
            rows,
            pltpu.VMEM((whole, width), bf16),
            pltpu.VMEM((pairs, LANES, own), f32),
            pltpu.VMEM((pairs, own, LANES), bf16),
            pltpu.VMEM((pairs, own, LANES), bf16),
            pltpu.VMEM((pairs, 2 * own, whole), bf16),
            pltpu.VMEM((pairs, 2 * own, whole), bf16),
            pltpu.VMEM((pairs, whole, 2 * own), bf16),
        ),
    )


def cross_backward(x, d_resid, lines, saved):
    slots = x.shape[0]
    toks, width = d_resid.shape
    return whole_call(
        back_kernel,
        "cross_backward",
        [
            shaped(PLANE * CHUNK, LANES, bf16),
            shaped(slots, LANES, bf16),
            shaped(toks, LANES, f32),
        ],
        (x, d_resid, lines) + tuple(saved),
        scratch=(
            pltpu.VMEM((slots, width), bf16),
            pltpu.VMEM((slots, LANES), f32),
            pltpu.VMEM((slots, LANES), bf16),
        ),
    )


def token_gradient(x, d_resid, lines, keys, d_raw, null_raw, w_query):
    return whole_call(
        token_kernel,
        "token_gradient",
        plain(*d_resid.shape, bf16),
        (x, d_resid, lines, d_raw, null_raw, keys, w_query),
        far=2,
        scratch=(
            pltpu.VMEM(keys.shape, bf16),
            pltpu.VMEM(w_query.shape, bf16),
            pltpu.SemaphoreType.DMA((2,)),
        ),
    )


def unpack(parts, width, scale):
    out = plain(FEATS, width, f32)
    return whole_call(
        functools.partial(unpack_kernel, scale), "unpack", [out, out], (parts,)
    )


def sum_everywhere(rows):
    plane = [list(range(z * PLANE, (z + 1) * PLANE)) for z in range(DEPTH)]
    lats = PLANE // 4
    column = [[z * lats + k for z in range(DEPTH)] for k in range(lats)]

    def swap(parts, axes, groups):
        return lax.all_to_all(
            parts, axes, split_axis=0, concat_axis=0, tiled=True, axis_index_groups=groups
        )

    def total(parts):
        return jnp.sum(parts.astype(f32), axis=0)

    parts = swap(rows.reshape(PLANE, CHUNK, LANES), ("lat", "lon"), plane)
    mine = total(parts).astype(bf16)
    parts = swap(jnp.broadcast_to(mine, (DEPTH, CHUNK, LANES)), "lat", column)
    mine = total(parts).astype(bf16)
    parts = swap(jnp.broadcast_to(mine, (PLANE, CHUNK, LANES)), ("lat", "lon"), plane)
    return parts.reshape(PLANE * CHUNK, LANES)


def on_device(
    tokens,
    cotangent,
    raw_obs,
    obs_band,
    obs_slot,
    obs_inst,
    obs_count,
    w_key_obs,
    w_val_obs,
    inst_table,
    null_key,
    null_val,
    w_query,
    norm_gain,
    zonal_query,
    zonal_key,
    zonal_value,
    zonal_out,
):
    tok_rows, width = tokens.shape[1:]
    bands = lax.axis_size("lat")
    devices = bands * lax.axis_size("lon")
    obs_total = raw_obs.shape[0] * devices
    tok = tokens.reshape(tok_rows, width)
    cot = cotangent.reshape(tok_rows, width)
    packed = pack(obs_count, obs_band, obs_slot, obs_inst, raw_obs, bands)
    received = lax.all_to_all(
        packed.reshape(bands, CAP_ROWS, LANES), "lat", split_axis=0, concat_axis=0, tiled=True
    ).reshape(bands * CAP_ROWS, LANES)
    d_att, query, lines = get_ready(
        tok, cot, w_query, zonal_out, null_key, null_val, norm_gain
    )
    att_all = lax.all_gather(d_att, "lon", axis=0, tiled=True)
    resid, normed, keys, *saved, lines, cot, zq, zk, zv, att_all = cross_forward(
        received,
        w_key_obs,
        w_val_obs,
        inst_table,
        query,
        lines,
        tok,
        cot,
        zonal_query,
        zonal_key,
        zonal_value,
        att_all,
    )
    normed_all = lax.all_gather(normed, "lon", axis=0, tiled=True)
    me = lax.axis_index("lon").astype(i32).reshape(1)
    d_resid = zonal(me, normed_all, att_all, zq, zk, zv, resid, cot, lines)
    grads, d_raw, null_raw = cross_backward(received, d_resid, lines, saved)
    d_tok = token_gradient(received, d_resid, lines, keys, d_raw, null_raw, w_query)
    key_grad, value_grad = unpack(sum_everywhere(grads), width, 1.0 / math.sqrt(obs_total))
    return d_tok.reshape(1, tok_rows, width), key_grad, value_grad


def solution(mesh):
    return jax.shard_map(
        on_device,
        mesh=mesh,
        in_specs=(
            P("lat", "lon", None),
            P("lat", "lon", None),
            P(("lat", "lon"), None),
            P(("lat", "lon"), None),
            P(("lat", "lon")),
            P(("lat", "lon")),
            P(("lat", "lon")),
            P(),
            P(),
            P(),
            P(),
            P(),
            P(),
            P(),
            P(),
            P(),
            P(),
            P(),
        ),
        out_specs=(P("lat", "lon", None), P(), P()),
        check_vma=False,
    )
```

```python
import functools
import math

import jax
import jax.numpy as jnp
from jax import lax
from jax.experimental import pallas as pl
from jax.experimental.pallas import tpu as pltpu
from jax.sharding import PartitionSpec as P

HEAD_DIM = 64
CAP_ROWS = 8
LANES = 128
FEATS = 64

logit_cap = 6.0
norm_eps = 1e-06
score_scale = 1.0 / math.sqrt(HEAD_DIM)
LOG2E = math.log2(math.e)

bf16 = jnp.bfloat16
f32 = jnp.float32
i32 = jnp.int32

PLANE = 32
DEPTH = 16
CHUNK = 24
ROW_BLOCK = 1024


def iota(shape, dim):
    return lax.broadcasted_iota(i32, shape, dim)


def dot_nn(a, b):
    return lax.dot_general(a, b, (((1,), (0,)), ((), ())), preferred_element_type=f32)


def dot_nt(a, b):
    return lax.dot_general(a, b, (((1,), (1,)), ((), ())), preferred_element_type=f32)


def dot_tn(a, b):
    return lax.dot_general(a, b, (((0,), (0,)), ((), ())), preferred_element_type=f32)


def halves(value):
    high = value.astype(bf16)
    return high, (value - high.astype(f32)).astype(bf16)


def fine_nn(twice, value):
    return dot_nn(twice, jnp.concatenate(halves(value), axis=0))


def fine_tn(a, value):
    both = dot_tn(a, jnp.concatenate(halves(value), axis=1))
    return both[:, : value.shape[1]] + both[:, value.shape[1] :]


def fine_nn_left(value, b):
    high, low = halves(value)
    return dot_nn(high, b) + dot_nn(low, b)


def doubled(hot):
    return jnp.concatenate([hot, hot], axis=1)


def head_sum_matrix(width):
    return jnp.where(
        iota((width, LANES), 0) // HEAD_DIM == iota((width, LANES), 1), 1.0, 0.0
    ).astype(bf16)


def head_spread_matrix(width):
    return jnp.where(
        iota((LANES, width), 1) // HEAD_DIM == iota((LANES, width), 0), 1.0, 0.0
    ).astype(bf16)


def token_hot(x_rows):
    slot = x_rows[:, FEATS : FEATS + 1].astype(f32).astype(i32)
    return jnp.where(iota((x_rows.shape[0], LANES), 1) == slot - 1, 1.0, 0.0).astype(bf16)


def pack_kernel(
    count_ref,
    band_hbm,
    slot_hbm,
    inst_hbm,
    raw_hbm,
    out_hbm,
    band_ref,
    slot_ref,
    inst_ref,
    raw_ref,
    out_ref,
    in_sems,
    out_sems,
):
    moves = [
        pltpu.make_async_copy(src, dst, in_sems.at[k])
        for k, (src, dst) in enumerate(
            (
                (band_hbm, band_ref),
                (raw_hbm, raw_ref),
                (slot_hbm, slot_ref),
                (inst_hbm, inst_ref),
            )
        )
    ]
    for move in moves:
        move.start()
    rows = band_ref.shape[1]
    slots = out_ref.shape[0]
    bands = slots // CAP_ROWS
    earlier = jnp.where(iota((rows, rows), 0) < iota((rows, rows), 1), 1.0, 0.0).astype(bf16)
    moves[0].wait()
    band = band_ref[...]
    live = iota((1, rows), 1) < count_ref[0]
    dest = jnp.where(live, band, -1)
    named = iota((bands, rows), 0) == dest
    hot = jnp.where(named, 1.0, 0.0).astype(bf16)
    before = dot_nn(hot, earlier)
    rank = jnp.sum(jnp.where(named, before, 0.0), axis=0, keepdims=True).astype(i32)
    position = jnp.where(live, band * CAP_ROWS + rank, -1)
    for move in moves[1:]:
        move.wait()
    part = iota((LANES - FEATS, rows), 0)
    meta = jnp.where(
        part == 0,
        (slot_ref[...] + 1).astype(f32),
        jnp.where(part == 1, inst_ref[...].astype(f32), 0.0),
    ).astype(bf16)
    payload = jnp.concatenate([raw_ref[...], meta], axis=0)
    step = slots // out_sems.shape[0]
    leaving = []
    for k in range(out_sems.shape[0]):
        span = pl.ds(k * step, step)
        pick = jnp.where(iota((step, rows), 0) + k * step == position, 1.0, 0.0).astype(bf16)
        out_ref[span, :] = dot_nt(pick, payload).astype(bf16)
        leaving.append(
            pltpu.make_async_copy(out_ref.at[span], out_hbm.at[span], out_sems.at[k])
        )
        leaving[-1].start()
    for move in leaving:
        move.wait()


def ready_kernel(
    tok_ref,
    cot_ref,
    wq_ref,
    zo_ref,
    nk_ref,
    nv_ref,
    gain_ref,
    att_ref,
    query_ref,
    lines_ref,
):
    att_ref[...] = dot_nt(cot_ref[...], zo_ref[...]).astype(bf16)
    query_ref[...] = dot_nn(tok_ref[...], wq_ref[...]).astype(bf16)
    lines_ref[...] = jnp.zeros(lines_ref.shape, f32)
    for row, ref in enumerate((nk_ref, nv_ref, gain_ref)):
        for k in range(ref.shape[0]):
            cols = slice(k * LANES, (k + 1) * LANES)
            lines_ref[row : row + 1, cols] = ref[k : k + 1, :].astype(f32)


def cross_kernel(
    x_ref,
    wk_ref,
    wv_ref,
    table_ref,
    query_ref,
    lines_ref,
    tok_ref,
    cot_ref,
    zq_ref,
    zk_ref,
    zv_ref,
    resid_ref,
    normed_ref,
    key_ref,
    val_ref,
    slope_ref,
    qs_ref,
    tanh_ref,
    prob_ref,
    ntanh_ref,
    nprob_ref,
    hot_s,
    wide_ref,
    lines_out,
    cot_out,
    zq_out,
    zk_out,
    zv_out,
    both_s,
    query_s,
    tok_s,
    keys_s,
    inst_s,
    weight_s,
    sems,
    key_sem,
):
    slots = x_ref.shape[0]
    feats, width = wk_ref.shape
    kinds = table_ref.shape[0]
    toks = tok_ref.shape[0]
    first = LANES + kinds
    moves = [
        pltpu.make_async_copy(src, dst, sems.at[k])
        for k, (src, dst) in enumerate(
            (
                (wk_ref, both_s.at[:feats, :width]),
                (wv_ref, both_s.at[:feats, width:]),
                (table_ref, both_s.at[LANES:first, width:]),
                (query_ref, query_s),
                (lines_ref, lines_out),
                (tok_ref, tok_s),
                (zq_ref, zq_out),
                (zk_ref, zk_out),
                (zv_ref, zv_out),
                (cot_ref, cot_out),
            )
        )
    ]
    for move in moves[:6]:
        move.start()
    both_s[feats:LANES, :] = jnp.zeros((LANES - feats, 2 * width), bf16)
    both_s[LANES:first, :width] = jnp.zeros((kinds, width), bf16)
    both_s[first:, :] = jnp.zeros((LANES - kinds, 2 * width), bf16)
    head_sum = head_sum_matrix(width)
    head_spread = head_spread_matrix(width)
    for start in range(0, slots, ROW_BLOCK):
        span = pl.ds(start, ROW_BLOCK)
        x = x_ref[span, :]
        hot_s[span, :] = token_hot(x)
        inst = x[:, FEATS + 1 : FEATS + 2].astype(f32).astype(i32)
        inst_s[span, :] = jnp.where(
            iota((ROW_BLOCK, LANES), 1) == inst, 1.0, 0.0
        ).astype(bf16)
    for move in moves[:4]:
        move.wait()
    for move in moves[6:]:
        move.start()
    w_both = both_s[...]
    query = query_s[...]
    total = jnp.zeros((toks, LANES), f32)
    for start in range(0, slots, ROW_BLOCK):
        span = pl.ds(start, ROW_BLOCK)
        hot = hot_s[span, :]
        encoded = dot_nn(jnp.concatenate([x_ref[span, :], inst_s[span, :]], axis=1), w_both)
        keys = encoded[:, :width].astype(bf16)
        keys_s[span, :] = keys
        pre = encoded[:, width:]
        sigma = 0.5 + 0.5 * jnp.tanh(0.5 * pre)
        val_ref[span, :] = (pre * sigma).astype(bf16)
        slope_ref[span, :] = (sigma * (1.0 + pre * (1.0 - sigma))).astype(bf16)
        q_slot = dot_nn(hot, query).astype(bf16)
        qs_ref[span, :] = q_slot
        t = jnp.tanh(dot_nn(q_slot * keys, head_sum) * (score_scale / logit_cap))
        tanh_ref[span, :] = t
        weight = jnp.exp(logit_cap * t)
        weight_s[span, :] = weight
        total = total + fine_tn(hot, weight)
    away = pltpu.make_async_copy(keys_s, key_ref, key_sem)
    away.start()
    for move in moves[4:6]:
        move.wait()
    null_key = lines_out[0:1, :]
    null_val = lines_out[1:2, :]
    gain = lines_out[2:3, :]
    null_t = jnp.tanh(
        fine_nn_left(query.astype(f32) * null_key, head_sum)
        * (score_scale / logit_cap)
    )
    null_weight = jnp.exp(logit_cap * null_t)
    share = 1.0 / (total + null_weight)
    null_prob = null_weight * share
    ntanh_ref[...] = null_t
    nprob_ref[...] = null_prob
    gathered = dot_nn(null_prob.astype(bf16), head_spread) * null_val
    for start in range(0, slots, ROW_BLOCK):
        span = pl.ds(start, ROW_BLOCK)
        hot = hot_s[span, :]
        prob = weight_s[span, :] * fine_nn(doubled(hot), share)
        prob_ref[span, :] = prob
        spread = dot_nn(prob.astype(bf16), head_spread).astype(bf16)
        wide_ref[span, :] = spread
        gathered = gathered + dot_tn(hot, spread * val_ref[span, :])
    resid = (tok_s[...].astype(f32) + gathered).astype(bf16)
    resid_ref[...] = resid
    resid_f = resid.astype(f32)
    inverse = lax.rsqrt(jnp.mean(resid_f * resid_f, axis=1, keepdims=True) + norm_eps)
    normed_ref[...] = (resid_f * inverse * gain).astype(bf16)
    for move in moves[6:]:
        move.wait()
    away.wait()


def zonal_kernel(
    me_ref,
    normed_ref,
    zq_ref,
    zk_ref,
    zv_ref,
    resid_ref,
    cot_ref,
    lines_ref,
    att_ref,
    dres_ref,
    zq_s,
    zk_s,
    zkt_s,
    zv_s,
    att_s,
    norm_s,
    dq_s,
    dk_s,
    dv_s,
    top_s,
    prob_s,
    col_s,
):
    whole, width = normed_ref.shape
    own = resid_ref.shape[0]
    sectors = whole // own
    pairs = width // LANES
    me = me_ref[0]
    for k in range(sectors):
        src = pl.multiple_of(lax.rem(me + k, sectors) * own, own)
        norm_s[k * own : (k + 1) * own, :] = normed_ref[pl.ds(src, own), :]
    normed = norm_s[...]
    for ref, out in ((zq_ref, zq_s), (zk_ref, zk_s), (zv_ref, zv_s)):
        proj = dot_nn(normed, ref[...])
        for p in range(pairs):
            piece = proj[:, p * LANES : (p + 1) * LANES]
            out[p] = piece.astype(bf16)
            if out is zk_s:
                zkt_s[p] = piece.astype(bf16).T
    for k in range(sectors):
        src = pl.multiple_of(lax.rem(me + k, sectors) * own, own)
        part = att_ref[pl.ds(src, own), :]
        for p in range(pairs):
            att_s[p, k * own : (k + 1) * own, :] = part[:, p * LANES : (p + 1) * LANES]
    lane_head = iota((whole, LANES), 1) // HEAD_DIM
    low_half = iota((own, LANES), 1) < HEAD_DIM

    def scores(p):
        keys = zk_s[p]
        vals = zv_s[p]
        for head in range(2):
            rows = slice(head * own, (head + 1) * own)
            qm = jnp.where(lane_head == head, zq_s[p], jnp.zeros((), bf16))
            am = jnp.where(lane_head == head, att_s[p], jnp.zeros((), bf16))
            half = whole // 2
            for start in (0, half):
                cols = slice(start, start + half)
                t = jnp.tanh(dot_nt(keys, qm[cols]) * (score_scale / logit_cap))
                zdp = dot_nt(vals, am[cols])
                weight = jnp.exp2((logit_cap * LOG2E) * t)
                share = 1.0 / jnp.sum(weight, axis=0, keepdims=True)
                inner = jnp.sum(weight * zdp, axis=0, keepdims=True) * share
                t_top = t[:own]
                prob = weight[:own] * share
                top = (prob * (zdp[:own] - inner) * (1.0 - t_top * t_top)).astype(bf16)
                top_s[p, rows, cols] = top
                prob_s[p, rows, cols] = prob.astype(bf16)
                if start == 0:
                    t_rest = t[own:, :own]
                    rest = (
                        (weight[own:, :own] * share[:, :own])
                        * (zdp[own:, :own] - inner[:, :own])
                        * (1.0 - t_rest * t_rest)
                    ).astype(bf16)
                    col_s[p, :own, rows] = top[:, :own]
                    col_s[p, own:, rows] = rest

    def gradients(p):
        dk = dot_nn(top_s[p], zq_s[p])
        dk_s[p] = (jnp.where(low_half, dk[:own], dk[own:]) * score_scale).astype(bf16)
        dv = dot_nn(prob_s[p], att_s[p])
        dv_s[p] = jnp.where(low_half, dv[:own], dv[own:]).astype(bf16)
        dq = dot_nn(zkt_s[p], col_s[p])
        dq_s[p, :HEAD_DIM, :] = dq[:HEAD_DIM, :own] * score_scale
        dq_s[p, HEAD_DIM:, :] = dq[HEAD_DIM:, own:] * score_scale

    for p in range(pairs):
        scores(p)
    for p in range(pairs):
        gradients(p)
    d_zq = jnp.concatenate([dq_s[p].T.astype(bf16) for p in range(pairs)], axis=1)
    d_zk = jnp.concatenate([dk_s[p] for p in range(pairs)], axis=1)
    d_zv = jnp.concatenate([dv_s[p] for p in range(pairs)], axis=1)
    d_normed = (
        dot_nt(d_zq, zq_ref[...]) + dot_nt(d_zk, zk_ref[...]) + dot_nt(d_zv, zv_ref[...])
    )
    resid_f = resid_ref[...].astype(f32)
    inverse = lax.rsqrt(jnp.mean(resid_f * resid_f, axis=1, keepdims=True) + norm_eps)
    gained = lines_ref[2:3, :] * d_normed
    dres_ref[...] = (
        cot_ref[...].astype(f32)
        + inverse * gained
        - resid_f * (inverse * inverse * inverse) * jnp.mean(resid_f * gained, axis=1, keepdims=True)
    ).astype(bf16)


def back_kernel(
    x_ref,
    dres_ref,
    lines_ref,
    val_ref,
    slope_ref,
    qs_ref,
    tanh_ref,
    prob_ref,
    ntanh_ref,
    nprob_ref,
    hot_s,
    wide_ref,
    grad_ref,
    draw_ref,
    nraw_ref,
    ds_s,
    dp_s,
):
    slots = x_ref.shape[0]
    toks, width = dres_ref.shape
    head_sum = head_sum_matrix(width)
    head_spread = head_spread_matrix(width)
    d_resid = dres_ref[...]
    null_prob = nprob_ref[...]
    null_t = ntanh_ref[...]
    null_dp = fine_nn_left(d_resid.astype(f32) * lines_ref[1:2, :], head_sum)
    inner = null_prob * null_dp
    for start in range(0, slots, ROW_BLOCK):
        span = pl.ds(start, ROW_BLOCK)
        hot = hot_s[span, :]
        d_slot = dot_nn(hot, d_resid).astype(bf16)
        ds_s[span, :] = d_slot
        dp = dot_nn(d_slot * val_ref[span, :], head_sum)
        dp_s[span, :] = dp
        inner = inner + fine_tn(hot, prob_ref[span, :] * dp)
    nraw_ref[...] = null_prob * (null_dp - inner) * (1.0 - null_t * null_t) * score_scale
    grads = jnp.zeros((LANES, 2 * width), f32)
    for start in range(0, slots, ROW_BLOCK):
        span = pl.ds(start, ROW_BLOCK)
        prob = prob_ref[span, :]
        t = tanh_ref[span, :]
        d_raw = (
            prob
            * (dp_s[span, :] - fine_nn(doubled(hot_s[span, :]), inner))
            * (1.0 - t * t)
            * score_scale
        ).astype(bf16)
        draw_ref[span, :] = d_raw
        d_raw_wide = dot_nn(d_raw, head_spread).astype(bf16)
        d_keys = d_raw_wide * qs_ref[span, :]
        d_pre = (wide_ref[span, :] * ds_s[span, :]) * slope_ref[span, :]
        grads = grads + dot_tn(x_ref[span, :], jnp.concatenate([d_keys, d_pre], axis=1))
    blocks = 2 * width // LANES
    for b in range(blocks):
        grad_ref[b * FEATS : (b + 1) * FEATS, :] = grads[
            :FEATS, b * LANES : (b + 1) * LANES
        ].astype(bf16)
    spare = grad_ref.shape[0] - blocks * FEATS
    grad_ref[blocks * FEATS :, :] = jnp.zeros((spare, LANES), bf16)


def token_kernel(
    hot_ref,
    dres_ref,
    lines_ref,
    draw_ref,
    nraw_ref,
    key_ref,
    wq_ref,
    dtok_ref,
    keys_s,
    wq_s,
    sems,
):
    slots = hot_ref.shape[0]
    keys_move = pltpu.make_async_copy(key_ref, keys_s, sems.at[0])
    wq_move = pltpu.make_async_copy(wq_ref, wq_s, sems.at[1])
    keys_move.start()
    wq_move.start()
    head_spread = head_spread_matrix(dres_ref.shape[1])
    d_query = fine_nn_left(nraw_ref[...], head_spread) * lines_ref[0:1, :]
    keys_move.wait()
    for start in range(0, slots, ROW_BLOCK):
        span = pl.ds(start, ROW_BLOCK)
        d_raw_wide = dot_nn(draw_ref[span, :], head_spread).astype(bf16)
        hot = hot_ref[span, :]
        d_query = d_query + dot_tn(hot, d_raw_wide * keys_s[span, :])
    wq_move.wait()
    d_tok = dres_ref[...].astype(f32) + dot_nt(d_query.astype(bf16), wq_s[...])
    dtok_ref[...] = d_tok.astype(bf16)


def in_vmem(value):
    return pltpu.with_memory_space_constraint(value, pltpu.VMEM)


def unpack_kernel(scale, parts_ref, key_ref, value_ref):
    width = key_ref.shape[1]
    pieces = width // LANES
    for g, out in enumerate((key_ref, value_ref)):
        for b in range(pieces):
            start = (g * pieces + b) * FEATS
            rows = parts_ref[start : start + FEATS, :].astype(f32)
            out[:, b * LANES : (b + 1) * LANES] = rows * scale


def in_hbm(value):
    return pltpu.with_memory_space_constraint(value, pltpu.HBM)


def whole_call(
    kernel, name, out_shape, args, scalars=0, fetched=0, far=0, away=(), scratch=(), scoped=16
):
    smem = pl.BlockSpec(memory_space=pltpu.SMEM)
    vmem = pl.BlockSpec(memory_space=pltpu.VMEM)
    hbm = pl.BlockSpec(memory_space=pltpu.HBM)
    several = isinstance(out_shape, (list, tuple))
    first, last = scalars + fetched, len(args) - far
    args = (
        tuple(args[:scalars])
        + tuple(in_hbm(a) for a in args[scalars:first])
        + tuple(in_vmem(a) for a in args[first:last])
        + tuple(in_hbm(a) for a in args[last:])
    )
    return pl.pallas_call(
        kernel,
        name=name,
        out_shape=out_shape,
        in_specs=[smem] * scalars + [vmem] * (last - scalars) + [hbm] * far,
        out_specs=[hbm if k in away else vmem for k in range(len(out_shape))]
        if several
        else vmem,
        scratch_shapes=list(scratch),
        compiler_params=pltpu.CompilerParams(vmem_limit_bytes=scoped * 1024 * 1024),
    )(*args)


def plain(rows, cols, dtype):
    return jax.ShapeDtypeStruct((rows, cols), dtype)


def shaped(rows, cols, dtype):
    return pltpu.VMEM((rows, cols), dtype)


def pack(obs_count, obs_band, obs_slot, obs_inst, raw_obs, bands):
    rows, feats = raw_obs.shape
    slots = bands * CAP_ROWS
    line = pltpu.VMEM((1, rows), i32)
    return whole_call(
        pack_kernel,
        "pack",
        [plain(slots, LANES, bf16)],
        (
            obs_count,
            obs_band.reshape(1, rows),
            obs_slot.reshape(1, rows),
            obs_inst.reshape(1, rows),
            raw_obs.T,
        ),
        scalars=1,
        far=4,
        away=(0,),
        scratch=(
            line,
            line,
            line,
            pltpu.VMEM((feats, rows), bf16),
            pltpu.VMEM((slots, LANES), bf16),
            pltpu.SemaphoreType.DMA((4,)),
            pltpu.SemaphoreType.DMA((4,)),
        ),
    )[0]


def get_ready(tok, cot, w_query, zonal_out, null_key, null_val, gain):
    toks, width = tok.shape
    args = (tok, cot, w_query, zonal_out) + tuple(
        v.reshape(width // LANES, LANES) for v in (null_key, null_val, gain)
    )
    return whole_call(
        ready_kernel,
        "get_ready",
        [
            plain(toks, width, bf16),
            pltpu.HBM((toks, width), bf16),
            pltpu.HBM((8, width), f32),
        ],
        args,
        fetched=len(args),
    )


def cross_forward(x, w_key, w_val, table, query, lines, tok, cot, zq, zk, zv):
    slots = x.shape[0]
    toks, width = tok.shape
    big = shaped(slots, width, bf16)
    small = shaped(slots, LANES, f32)
    null = shaped(toks, LANES, f32)
    row = shaped(toks, width, bf16)
    square = shaped(*zq.shape, bf16)
    far = (w_key, w_val, table, query, lines, tok, cot, zq, zk, zv)
    return whole_call(
        cross_kernel,
        "cross_forward",
        [row, row, pltpu.HBM((slots, width), bf16), big, big, big, small, small, null, null]
        + [shaped(slots, LANES, bf16), big]
        + [shaped(*lines.shape, f32), row, square, square, square],
        (x,) + far,
        far=len(far),
        away=(2,),
        scratch=(
            pltpu.VMEM((2 * LANES, 2 * width), bf16),
            pltpu.VMEM((toks, width), bf16),
            pltpu.VMEM((toks, width), bf16),
            pltpu.VMEM((slots, width), bf16),
            pltpu.VMEM((slots, LANES), bf16),
            pltpu.VMEM((slots, LANES), f32),
            pltpu.SemaphoreType.DMA((len(far),)),
            pltpu.SemaphoreType.DMA(()),
        ),
    )


def zonal(me, normed_all, att_all, zq, zk, zv, resid, cot, lines):
    own, width = resid.shape
    whole = normed_all.shape[0]
    pairs = width // LANES
    rows = pltpu.VMEM((pairs, whole, LANES), bf16)
    return whole_call(
        zonal_kernel,
        "zonal",
        shaped(own, width, bf16),
        (me, normed_all, zq, zk, zv, resid, cot, lines, att_all),
        scalars=1,
        scratch=(
            rows,
            rows,
            pltpu.VMEM((pairs, LANES, whole), bf16),
            rows,
            rows,
            pltpu.VMEM((whole, width), bf16),
            pltpu.VMEM((pairs, LANES, own), f32),
            pltpu.VMEM((pairs, own, LANES), bf16),
            pltpu.VMEM((pairs, own, LANES), bf16),
            pltpu.VMEM((pairs, 2 * own, whole), bf16),
            pltpu.VMEM((pairs, 2 * own, whole), bf16),
            pltpu.VMEM((pairs, whole, 2 * own), bf16),
        ),
    )


def cross_backward(x, d_resid, lines, saved, hot, wide):
    slots = x.shape[0]
    toks, width = d_resid.shape
    return whole_call(
        back_kernel,
        "cross_backward",
        [
            shaped(PLANE * CHUNK, LANES, bf16),
            shaped(slots, LANES, bf16),
            shaped(toks, LANES, f32),
        ],
        (x, d_resid, lines) + tuple(saved) + (hot, wide),
        scratch=(
            pltpu.VMEM((slots, width), bf16),
            pltpu.VMEM((slots, LANES), f32),
        ),
    )


def token_gradient(hot, d_resid, lines, keys, d_raw, null_raw, w_query):
    return whole_call(
        token_kernel,
        "token_gradient",
        plain(*d_resid.shape, bf16),
        (hot, d_resid, lines, d_raw, null_raw, keys, w_query),
        far=2,
        scratch=(
            pltpu.VMEM(keys.shape, bf16),
            pltpu.VMEM(w_query.shape, bf16),
            pltpu.SemaphoreType.DMA((2,)),
        ),
    )


def unpack(parts, width, scale):
    out = plain(FEATS, width, f32)
    return whole_call(
        functools.partial(unpack_kernel, scale), "unpack", [out, out], (parts,)
    )


def sum_everywhere(rows):
    plane = [list(range(z * PLANE, (z + 1) * PLANE)) for z in range(DEPTH)]
    lats = PLANE // 4
    column = [[z * lats + k for z in range(DEPTH)] for k in range(lats)]

    def swap(parts, axes, groups):
        return lax.all_to_all(
            parts, axes, split_axis=0, concat_axis=0, tiled=True, axis_index_groups=groups
        )

    def total(parts):
        return jnp.sum(parts.astype(f32), axis=0)

    parts = swap(rows.reshape(PLANE, CHUNK, LANES), ("lat", "lon"), plane)
    mine = total(parts).astype(bf16)
    parts = swap(jnp.broadcast_to(mine, (DEPTH, CHUNK, LANES)), "lat", column)
    mine = total(parts).astype(bf16)
    parts = swap(jnp.broadcast_to(mine, (PLANE, CHUNK, LANES)), ("lat", "lon"), plane)
    return parts.reshape(PLANE * CHUNK, LANES)


def on_device(
    tokens,
    cotangent,
    raw_obs,
    obs_band,
    obs_slot,
    obs_inst,
    obs_count,
    w_key_obs,
    w_val_obs,
    inst_table,
    null_key,
    null_val,
    w_query,
    norm_gain,
    zonal_query,
    zonal_key,
    zonal_value,
    zonal_out,
):
    tok_rows, width = tokens.shape[1:]
    bands = lax.axis_size("lat")
    devices = bands * lax.axis_size("lon")
    obs_total = raw_obs.shape[0] * devices
    tok = tokens.reshape(tok_rows, width)
    cot = cotangent.reshape(tok_rows, width)
    packed = pack(obs_count, obs_band, obs_slot, obs_inst, raw_obs, bands)
    received = lax.all_to_all(
        packed.reshape(bands, CAP_ROWS, LANES), "lat", split_axis=0, concat_axis=0, tiled=True
    ).reshape(bands * CAP_ROWS, LANES)
    d_att, query, lines = get_ready(
        tok, cot, w_query, zonal_out, null_key, null_val, norm_gain
    )
    att_all = lax.all_gather(d_att, "lon", axis=0, tiled=True)
    resid, normed, keys, *saved, hot, wide, lines, cot, zq, zk, zv = cross_forward(
        received,
        w_key_obs,
        w_val_obs,
        inst_table,
        query,
        lines,
        tok,
        cot,
        zonal_query,
        zonal_key,
        zonal_value,
    )
    normed_all = lax.all_gather(normed, "lon", axis=0, tiled=True)
    me = lax.axis_index("lon").astype(i32).reshape(1)
    d_resid = zonal(me, normed_all, att_all, zq, zk, zv, resid, cot, lines)
    grads, d_raw, null_raw = cross_backward(received, d_resid, lines, saved, hot, wide)
    d_tok = token_gradient(hot, d_resid, lines, keys, d_raw, null_raw, w_query)
    key_grad, value_grad = unpack(sum_everywhere(grads), width, 1.0 / math.sqrt(obs_total))
    return d_tok.reshape(1, tok_rows, width), key_grad, value_grad


def solution(mesh):
    return jax.shard_map(
        on_device,
        mesh=mesh,
        in_specs=(
            P("lat", "lon", None),
            P("lat", "lon", None),
            P(("lat", "lon"), None),
            P(("lat", "lon"), None),
            P(("lat", "lon")),
            P(("lat", "lon")),
            P(("lat", "lon")),
            P(),
            P(),
            P(),
            P(),
            P(),
            P(),
            P(),
            P(),
            P(),
            P(),
            P(),
        ),
        out_specs=(P("lat", "lon", None), P(), P()),
        check_vma=False,
    )
```
